32 devices in a mesh: gz: 4 (over z), gy: 4 (over x, core), gx: 2 (over y).
Axes of the slice: x: 2, y: 2, z: 4, core: 2. Of those that a mesh axis runs over, the one named last changes fastest.
Arguments:
- stacks: bfloat16 [32, 32, 512], P('gz', 'gy', 'gx'), may hold values from -6 to 6
- offsets: int32 [2], replicated, may hold values from -32 to 32, as said below
- ramp_width: int32 [2], replicated, may hold values from 17 to 64, as said below
- stem_weight: bfloat16 [27, 32], replicated, may hold values from -1.25 to 1.25
- stem_bias: float32 [32], replicated, may hold values from -3 to 3
- layer_weight: bfloat16 [4, 27, 32, 32], replicated, may hold values from -0.21875 to 0.21875
- layer_bias: float32 [4, 32], replicated, may hold values from -3 to 3
- head_weight: bfloat16 [32], replicated, may hold values from -1 to 1
Outputs:
- logits: float32 [32, 32, 256], P('gz', 'gy', 'gx')
The draws below stay inside these ranges and needn't reach their ends.
Inputs may be any that keep to these rules, and one draw needn't show every extreme that they name: `offsets`: each tile stack's shift; in every draw some stack is shifted by 32. `ramp_width`: each tile stack's ramp width; in every draw some stack has width 64 // 4 + 1 and another width 64.
All inputs are finite; a program needn't handle non-finite values.
Results may differ from the reference program's by a relative error of at most 0.0096.
Values may be sent and summed in bfloat16 or wider, within the bound.
No kernel may reach another device: no remote copies, remote signals or barrier semaphores. Data moves between devices by JAX's collectives and lax.ppermute only.
A program may use at most 128 MiB of HBM per device.

```python
import jax
import jax.numpy as jnp
from jax import lax

C = 32
LAYERS = 4
H = 64
S = 32
BX = 128
TW = 256
NTILES = 2
NZ = 32
NY = 32
NX = 256


def draw_offsets(key, part):
    first, second = jax.random.split(jax.random.fold_in(key, 11), 2)
    shifts = jax.random.randint(first, (NTILES,), -S, S + 1)
    highest = jax.random.randint(second, (), 0, NTILES)
    return shifts.at[highest].set(S).astype(jnp.int32)


def draw_ramp_width(key, part):
    first, second = jax.random.split(jax.random.fold_in(key, 23), 2)
    narrow = H // 4 + 1
    widths = jax.random.randint(first, (NTILES,), narrow, H + 1)
    chosen = jax.random.randint(second, (), 0, NTILES)
    following = (chosen + 1) % NTILES
    return widths.at[chosen].set(narrow).at[following].set(H).astype(jnp.int32)


def steps_of(stream_key, extent, cuts, low, top_value):
    def one(dim, parts):
        heights = jax.random.uniform(jax.random.fold_in(jax.random.fold_in(stream_key, 6), dim), (parts,), jnp.float32, low / len(cuts), top_value / len(cuts))
        return jnp.repeat(jnp.exp(heights), extent[dim] // parts).reshape((-1,) + (1,) * (len(extent) - dim - 1))

    factor_of = one(*cuts[0])
    for cut in cuts[1:]:
        factor_of = factor_of * one(*cut)
    return factor_of


def normal_values(rng, dims, scale, most, cuts=(), held_as=jnp.bfloat16):
    array = jax.random.normal(rng, dims, jnp.float32) * scale
    if len(cuts) > 0:
        array = steps_of(rng, dims, cuts, -0.22, 0.18) * array
    return jnp.clip(array, min=-most, max=most).astype(held_as)


def setup_inputs(seed: int = 0) -> dict:
    arg_keys = jax.random.split(jax.random.key(seed), 9)
    return {
        "stacks": normal_values(arg_keys[0], (NZ, NY, NTILES * TW), 1.0, 6.0, ((0, 4), (1, 4), (2, 2))),
        "offsets": draw_offsets(jax.random.fold_in(arg_keys[8], 71), 0),
        "ramp_width": draw_ramp_width(jax.random.fold_in(arg_keys[8], 71), 0),
        "stem_weight": normal_values(arg_keys[3], (27, C), 27 ** -0.5, 1.25),
        "stem_bias": normal_values(arg_keys[4], (C,), 0.5, 3.0, (), jnp.float32),
        "layer_weight": normal_values(arg_keys[5], (LAYERS, 27, C, C), (27 * C) ** -0.5, 0.21875),
        "layer_bias": normal_values(arg_keys[6], (LAYERS, C), 0.3, 3.0, (), jnp.float32),
        "head_weight": normal_values(arg_keys[7], (C,), C ** -0.5, 1.0),
    }


def blend_weight(position, width):
    return jnp.minimum(1.0, jnp.minimum((position + 1.0) / width, (TW - position) / width))


def dilated_conv(volume, kernel, spacing):
    return lax.conv_general_dilated(volume, kernel, (1, 1, 1), [(spacing, spacing)] * 3, rhs_dilation=(spacing, spacing, spacing), dimension_numbers=("NCDHW", "OIDHW", "NCDHW"), precision=lax.Precision.HIGHEST)


def reference(stacks, offsets, ramp_width, stem_weight, stem_bias, layer_weight, layer_bias, head_weight):
    margin = H + S
    numerator = jnp.zeros((NZ, NY, NX + 2 * margin), jnp.float32)
    denominator = jnp.zeros((NX + 2 * margin,), jnp.float32)
    columns = jnp.arange(TW).astype(jnp.float32)
    anchor = jnp.zeros((), jnp.int32)
    for tile_idx in range(NTILES):
        start_col = (tile_idx * BX - H + margin + offsets[tile_idx]).astype(jnp.int32)
        weights = blend_weight(columns, ramp_width[tile_idx].astype(jnp.float32))
        weighted = stacks[:, :, tile_idx * TW:(tile_idx + 1) * TW].astype(jnp.float32) * weights
        current = lax.dynamic_slice(numerator, (anchor, anchor, start_col), (NZ, NY, TW))
        numerator = lax.dynamic_update_slice(numerator, current + weighted, (anchor, anchor, start_col))
        current_w = lax.dynamic_slice(denominator, (start_col,), (TW,))
        denominator = lax.dynamic_update_slice(denominator, current_w + weights, (start_col,))
    blended = numerator[:, :, margin:margin + NX] / denominator[margin:margin + NX]
    stem_kernel = stem_weight.astype(jnp.float32).T.reshape(C, 1, 3, 3, 3)
    stem_out = dilated_conv(blended[None, None], stem_kernel, 1)[0]
    features = jax.nn.relu(stem_out + stem_bias[:, None, None, None]).astype(jnp.bfloat16)
    for layer_idx in range(LAYERS):
        kernel = jnp.transpose(layer_weight[layer_idx].astype(jnp.float32), (1, 2, 0)).reshape(C, C, 3, 3, 3)
        conv_out = dilated_conv(features.astype(jnp.float32)[None], kernel, 2 ** layer_idx)[0]
        conv_out = conv_out + layer_bias[layer_idx][:, None, None, None]
        features = (features.astype(jnp.float32) + jax.nn.relu(conv_out)).astype(jnp.bfloat16)
    return jnp.einsum("c,czyx->zyx", head_weight.astype(jnp.float32), features.astype(jnp.float32), precision=lax.Precision.HIGHEST)
```

```python
import jax
import jax.numpy as jnp
from jax import lax
from jax.experimental import pallas as pl
from jax.experimental.pallas import tpu as pltpu
from jax.sharding import PartitionSpec as P

LAYERS = 4
H = 64
S = 32
BX = 128
C = 32
REACH = 16
SLAB = 8
WIDE = SLAB + 2 * REACH
NZ = 32
NY = 32
GROUPS = (10, 9, 8, 6, 2)
TAPS = (2, 2, 3, 3)
STEP = (1, 1, 1, 2)
ORIGIN = (-15, -14, -12, -8, 0)
BF = jnp.bfloat16
F32 = jnp.float32


def blend_weight(position, width, tile_len):
    spot = position.astype(F32)
    return jnp.minimum(1.0, jnp.minimum((spot + 1.0) / width, (tile_len - spot) / width))


def table_entry(table, wanted):
    slots = jnp.arange(table.shape[0])
    return jnp.sum(jnp.where(slots == wanted, table, 0))


def weights_kernel(lw_ref, sw_ref, ws_ref, *w_refs):
    lane = lax.broadcasted_iota(jnp.int32, (C, 4 * C), 1) // C
    zero = jnp.zeros((C, 4 * C), BF)
    for layer in range(LAYERS):
        spacing = 2**layer
        out = w_refs[layer]

        def per_row_tap(s, carry, layer=layer, spacing=spacing, out=out):
            taps = [
                [lw_ref[layer, 9 * c + a + 3 * s].astype(F32) for a in range(3)] for c in range(3)
            ]
            for i in range(TAPS[layer]):
                for xi in range(4):
                    rows = pl.ds(xi * C, C)
                    for c in range(3):
                        block = jnp.zeros((C, 4 * C), F32)
                        for a in range(3):
                            xo = 4 * STEP[layer] * i + xi - spacing * a
                            if 0 <= xo < 4:
                                block = jnp.where(lane == xo, taps[c][a], block)
                        block = block.astype(BF)
                        out[s, i, c, rows, 0 : 4 * C] = block
                        out[s, i, c + 1, rows, 4 * C : 8 * C] = block
                    out[s, i, 0, rows, 4 * C : 8 * C] = zero
                    out[s, i, 3, rows, 0 : 4 * C] = zero
            return carry

        lax.fori_loop(0, 3, per_row_tap, 0)
    row = lax.broadcasted_iota(jnp.int32, (128, 8 * C), 0)
    column = lax.broadcasted_iota(jnp.int32, (128, 8 * C), 1) // C

    def per_tile(k, carry):
        diff = row - column - 8 * k
        for c in range(3):
            block = jnp.zeros((128, 8 * C), F32)
            for b in range(3):
                for a in range(3):
                    tap = 9 * c + 3 * b + a
                    block = jnp.where(diff == WIDE * b + a, sw_ref[tap : tap + 1, :], block)
            ws_ref[k, 128 * c : 128 * (c + 1), :] = block.astype(BF)
        return carry

    lax.fori_loop(0, GROUPS[0] // 2, per_tile, 0)


def shifted(value, by):
    rows = value.shape[0]
    spot = lax.broadcasted_iota(jnp.int32, value.shape, 0) % NY
    moved = pltpu.roll(value, by % rows, 0)
    keep = (spot >= by) if by > 0 else (spot < NY + by)
    return jnp.where(keep, moved, 0.0)


def conv_kernel(
    cols_ref, image_ref, ws_ref, w0, w1, w2, w3, sb_ref, lb_ref, head_ref, out_ref, stem_in, *acts
):
    w_refs = (w0, w1, w2, w3)
    first_col = cols_ref[0]
    total_cols = cols_ref[1]

    def col_mask(layer, group, width):
        lane = lax.broadcasted_iota(jnp.int32, (1, width * C), 1) // C
        col = lane + (4 * group + first_col + ORIGIN[layer])
        return jnp.where((col >= 0) & (col < total_cols), 1.0, 0.0)

    for layer in range(LAYERS):
        spacing = 2**layer
        pad = jnp.zeros((3, spacing, NY, 4 * C), BF)
        for g in range(GROUPS[layer]):
            acts[layer][:, g, 1, :, 0] = pad
            acts[layer][:, g, 0, :, NZ // (2 * spacing) + 1] = pad

    image = image_ref[...].astype(F32).reshape(NZ * NY, WIDE)
    stem_in[...] = jnp.zeros(stem_in.shape, BF)
    blank = jnp.zeros((NZ * NY, 128 - 3 * WIDE), F32)
    packed = jnp.concatenate([shifted(image, 1), image, shifted(image, -1), blank], axis=1)
    stem_in[1 : NZ + 1] = packed.astype(BF).reshape(NZ, NY, 128)

    def store(layer, group, plane_sets):
        spacing = 2**layer
        for lead, value in plane_sets:
            for s in range(3):
                part = value if s == 1 else shifted(value, spacing if s == 0 else -spacing)
                planes = part.astype(BF).reshape(lead[1], NZ // (2 * spacing), 2, NY, 4 * C)
                for b in range(2):
                    acts[layer][
                        s, group, b, lead[0] : lead[0] + lead[1], 1 : 1 + NZ // (2 * spacing)
                    ] = planes[:, :, b]

    def stem_tile(k, carry):
        lhs = jnp.concatenate(
            [stem_in[c : c + NZ].reshape(NZ * NY, 128) for c in range(3)], axis=1
        )
        acc = jnp.dot(lhs, ws_ref[k], preferred_element_type=F32)
        acc = jnp.maximum(acc + sb_ref[...], 0.0) * col_mask(0, 2 * k, 8)
        store(0, 2 * k, [((0, 1), acc[:, : 4 * C])])
        store(0, 2 * k + 1, [((0, 1), acc[:, 4 * C :])])
        return carry

    lax.fori_loop(0, GROUPS[0] // 2, stem_tile, 0)

    for layer in range(LAYERS):
        spacing = 2**layer
        count = NZ // (2 * spacing)
        src = acts[layer]

        def conv_group(g, carry, layer=layer, spacing=spacing, count=count, src=src):
            pieces = []
            for s in range(3):
                for i in range(TAPS[layer]):
                    for t in range(4):
                        piece = src[
                            s,
                            g + STEP[layer] * i,
                            1 - t % 2,
                            :,
                            (t + 1) // 2 : (t + 1) // 2 + count,
                        ]
                        pieces.append(piece.reshape(NZ * NY // 2, 4 * C))
            lhs = jnp.concatenate(pieces, axis=1)
            weights = w_refs[layer][...].reshape(3 * TAPS[layer] * 4 * 128, 8 * C)
            acc = jnp.dot(lhs, weights, preferred_element_type=F32)
            mask = col_mask(layer + 1, g, 4)
            halves = []
            for b in range(2):
                if layer < 2:
                    pair = jnp.concatenate(
                        [
                            src[1, g + i, b, :, 1 : 1 + count].reshape(NZ * NY // 2, 4 * C)
                            for i in range(2)
                        ],
                        axis=1,
                    ).astype(F32)
                    centre = pair[:, spacing * C : spacing * C + 4 * C]
                else:
                    centre = src[1, g + STEP[layer], b, :, 1 : 1 + count]
                    centre = centre.reshape(NZ * NY // 2, 4 * C).astype(F32)
                half = acc[:, 4 * C * b : 4 * C * (b + 1)] + lb_ref[layer]
                halves.append(centre + jnp.maximum(half, 0.0) * mask)
            if layer + 1 < LAYERS:
                store(layer + 1, g, [((spacing * b, spacing), halves[b]) for b in range(2)])
            else:
                last = jnp.concatenate(halves, axis=1).astype(BF)
                out_ref[g] = lax.dot_general(
                    head_ref[...], last, (((1,), (1,)), ((), ())), preferred_element_type=F32
                )
            return carry

        lax.fori_loop(0, GROUPS[layer + 1], conv_group, 0)


def vmem():
    return pl.BlockSpec(memory_space=pltpu.VMEM)


def body(
    stacks, offsets, ramp_width, stem_weight, stem_bias, layer_weight, layer_bias, head_weight
):
    depth_b, rows_b, tile_len = stacks.shape
    depth_parts, row_parts = lax.axis_size("gz"), lax.axis_size("gy")
    parts = depth_parts * row_parts
    column_idx = lax.axis_index("gx")
    column_cnt = lax.axis_size("gx")
    slab_idx = lax.axis_index("gz") * row_parts + lax.axis_index("gy")
    assert (depth_b * depth_parts, rows_b * row_parts, parts * SLAB) == (NZ, NY, BX)

    edge = H + S + REACH
    low_end = stacks[:, :, tile_len - edge :]
    high_end = stacks[:, :, :edge]
    if column_cnt == 2:
        got = lax.ppermute(jnp.where(column_idx == 0, low_end, high_end), "gx", [(0, 1), (1, 0)])
        from_lower, from_upper = got, got
    else:
        forward = [(i, i + 1) for i in range(column_cnt - 1)]
        from_lower = lax.ppermute(low_end, "gx", forward)
        from_upper = lax.ppermute(high_end, "gx", [(b, a) for a, b in forward])

    tiled = jnp.tile(jnp.swapaxes(layer_weight, 2, 3), (1, 1, 1, 4))
    stem_tiled = jnp.tile(stem_weight.astype(F32), (1, 8))
    shapes = [jax.ShapeDtypeStruct((GROUPS[0] // 2, 384, 8 * C), BF)] + [
        jax.ShapeDtypeStruct((3, TAPS[layer], 4, 4 * C, 8 * C), BF) for layer in range(LAYERS)
    ]
    weights = pl.pallas_call(
        weights_kernel,
        out_shape=shapes,
        in_specs=[vmem(), vmem()],
        out_specs=[vmem()] * 5,
        compiler_params=pltpu.CompilerParams(vmem_limit_bytes=40 * 2**20),
        cost_estimate=pl.CostEstimate(flops=4000000, bytes_accessed=9000000, transcendentals=0),
    )(tiled, stem_tiled)

    shift_own = table_entry(offsets, column_idx)
    shift_lower = table_entry(offsets, column_idx - 1)
    shift_upper = table_entry(offsets, column_idx + 1)
    ramp_own = table_entry(ramp_width, column_idx).astype(F32)
    ramp_lower = table_entry(ramp_width, column_idx - 1).astype(F32)
    ramp_upper = table_entry(ramp_width, column_idx + 1).astype(F32)
    ramp_lower = jnp.where(column_idx > 0, ramp_lower, 1.0)
    ramp_upper = jnp.where(column_idx < column_cnt - 1, ramp_upper, 1.0)
    span = BX + 2 * REACH
    columns = jnp.arange(span) - REACH
    filler = jnp.zeros((depth_b, rows_b, span), BF)
    own_vals = lax.dynamic_slice_in_dim(stacks, H - REACH - shift_own, span, 2).astype(F32)
    lower_vals = lax.dynamic_slice_in_dim(
        jnp.concatenate([from_lower, filler], 2), S - shift_lower, span, 2
    ).astype(F32)
    upper_vals = lax.dynamic_slice_in_dim(
        jnp.concatenate([filler, from_upper], 2), H + REACH - shift_upper, span, 2
    ).astype(F32)
    weight_own = blend_weight(columns + H - shift_own, ramp_own, tile_len)
    lower_pos = columns + BX + H - shift_lower
    weight_lower = jnp.where(
        (lower_pos < tile_len) & (column_idx > 0),
        blend_weight(lower_pos, ramp_lower, tile_len),
        0.0,
    )
    upper_pos = columns - BX + H - shift_upper
    weight_upper = jnp.where(
        (upper_pos >= 0) & (column_idx < column_cnt - 1),
        blend_weight(upper_pos, ramp_upper, tile_len),
        0.0,
    )
    numerator = own_vals * weight_own + lower_vals * weight_lower + upper_vals * weight_upper
    blended = numerator / (weight_own + weight_lower + weight_upper)
    global_col = columns + column_idx * BX
    blended = jnp.where((global_col >= 0) & (global_col < column_cnt * BX), blended, 0.0)
    blended = blended.astype(BF)
    slabs = jnp.stack([blended[:, :, SLAB * j : SLAB * j + WIDE] for j in range(parts)])
    slabs = lax.all_to_all(slabs, ("gz", "gy"), 0, 0, tiled=True)
    image = slabs.reshape(depth_parts, row_parts, depth_b, rows_b, WIDE)
    image = image.transpose(0, 2, 1, 3, 4).reshape(NZ, NY, WIDE)

    cols = jnp.stack([column_idx * BX + slab_idx * SLAB, column_cnt * BX]).astype(jnp.int32)
    stem_bias_row = jnp.tile(stem_bias[None], (1, 8))
    bias_rows = jnp.tile(layer_bias[:, None], (1, 1, 4))
    head_rows = jnp.kron(jnp.eye(8, dtype=F32), head_weight.astype(F32)[None]).astype(BF)
    scratch = [pltpu.VMEM((NZ + 2, NY, 128), BF)] + [
        pltpu.VMEM((3, GROUPS[layer], 2, 2**layer, NZ // 2 ** (layer + 1) + 2, NY, 4 * C), BF)
        for layer in range(LAYERS)
    ]
    flat = pl.pallas_call(
        conv_kernel,
        out_shape=jax.ShapeDtypeStruct((2, 8, NZ * NY // 2), F32),
        in_specs=[pl.BlockSpec(memory_space=pltpu.SMEM)] + [vmem()] * 9,
        out_specs=vmem(),
        scratch_shapes=scratch,
        compiler_params=pltpu.CompilerParams(vmem_limit_bytes=60 * 2**20),
        cost_estimate=pl.CostEstimate(
            flops=20000000000, bytes_accessed=9000000, transcendentals=0
        ),
    )(cols, image, *weights, stem_bias_row, bias_rows, head_rows)

    pieces = flat.reshape(2, 2, 4, 8, 2, row_parts, rows_b).transpose(4, 1, 5, 0, 2, 3, 6)
    pieces = pieces.reshape(parts, SLAB, depth_b * rows_b)
    pieces = lax.all_to_all(pieces, ("gz", "gy"), 0, 0, tiled=True)
    return pieces.reshape(BX, depth_b * rows_b).T.reshape(depth_b, rows_b, BX)


def solution(mesh):
    return jax.shard_map(
        body,
        mesh=mesh,
        in_specs=(P("gz", "gy", "gx"), P(), P(), P(), P(), P(), P(), P()),
        out_specs=P("gz", "gy", "gx"),
        check_vma=False,
    )
```

```python
import functools

import jax
import jax.numpy as jnp
from jax import lax
from jax.experimental import pallas as pl
from jax.experimental.pallas import tpu as pltpu
from jax.sharding import PartitionSpec as P

LAYERS = 4
H = 64
S = 32
BX = 128
C = 32
REACH = 16
SLAB = 8
WIDE = SLAB + 2 * REACH
NZ = 32
NY = 32
GROUPS = (10, 9, 8, 6, 2)
TAPS = (2, 2, 3, 3)
STEP = (1, 1, 1, 2)
ORIGIN = (-15, -14, -12, -8, 0)
BF = jnp.bfloat16
F32 = jnp.float32


def repeated(row, copies):
    return jnp.concatenate([row] * copies, axis=1)


def weights_kernel(
    lw_ref, lb_ref, sw_ref, sb_ref, head_ref, rows_ref, ws_ref, w0, w1, w2, w3, turned
):
    w_refs = (w0, w1, w2, w3)
    lane = lax.broadcasted_iota(jnp.int32, (C, 4 * C), 1) // C
    zero = jnp.zeros((C, 4 * C), BF)
    for layer in range(LAYERS):
        spacing = 2**layer
        out = w_refs[layer]
        flat = lw_ref[layer].astype(F32).reshape(27 * C, C)
        flat = jnp.concatenate([flat, jnp.zeros((28 * 4 * C - 27 * C, C), F32)], axis=0)
        flat = jnp.concatenate([flat, jnp.zeros((28 * 4 * C, 3 * C), F32)], axis=1)
        for t in range(27):
            turned[t] = flat[C * t : C * t + 4 * C].T[:C]

        def per_row_tap(s, carry, layer=layer, spacing=spacing, out=out):
            taps = []
            for c in range(3):
                taps.append([])
                for a in range(3):
                    block = jnp.where(lane == 0, turned[9 * c + a + 3 * s], 0.0)
                    block = block + pltpu.roll(block, 2 * C, 1)
                    taps[c].append(block + pltpu.roll(block, C, 1))
            for i in range(TAPS[layer]):
                for xi in range(4):
                    rows = pl.ds(xi * C, C)
                    for c in range(3):
                        block = jnp.zeros((C, 4 * C), F32)
                        for a in range(3):
                            xo = 4 * STEP[layer] * i + xi - spacing * a
                            if 0 <= xo < 4:
                                block = jnp.where(lane == xo, taps[c][a], block)
                        block = block.astype(BF)
                        out[s, i, c, rows, 0 : 4 * C] = block
                        out[s, i, c + 1, rows, 4 * C : 8 * C] = block
                    out[s, i, 0, rows, 4 * C : 8 * C] = zero
                    out[s, i, 3, rows, 0 : 4 * C] = zero
            return carry

        lax.fori_loop(0, 3, per_row_tap, 0)
    row = lax.broadcasted_iota(jnp.int32, (128, 8 * C), 0)
    column = lax.broadcasted_iota(jnp.int32, (128, 8 * C), 1) // C
    stem = repeated(sw_ref[...].astype(F32), 8)

    def per_tile(k, carry):
        diff = row - column - 8 * k
        for c in range(3):
            block = jnp.zeros((128, 8 * C), F32)
            for b in range(3):
                for a in range(3):
                    tap = 9 * c + 3 * b + a
                    block = jnp.where(diff == WIDE * b + a, stem[tap : tap + 1, :], block)
            ws_ref[k, 128 * c : 128 * (c + 1), :] = block.astype(BF)
        return carry

    lax.fori_loop(0, GROUPS[0] // 2, per_tile, 0)
    rows_ref[...] = jnp.zeros(rows_ref.shape, F32)
    rows_ref[0:1, :] = repeated(sb_ref[...], 8)
    for layer in range(LAYERS):
        rows_ref[8 + layer : 9 + layer, :] = repeated(lb_ref[layer : layer + 1], 8)
    head = repeated(head_ref[...].astype(F32), 8)
    spot = lax.broadcasted_iota(jnp.int32, (8, 8 * C), 0)
    rows_ref[16:24, :] = jnp.where(spot == column[:8], head, 0.0)


def pack_kernel(off_ref, stacks_ref, out_ref, *, parts, bricks):
    brick = lax.axis_index("gx")
    tile_len = stacks_ref.shape[2]
    rows = out_ref.shape[1]
    values = stacks_ref[...].astype(F32).reshape(2 * rows, tile_len)
    lane = lax.broadcasted_iota(jnp.int32, (rows, 128), 1)
    for other in range(bricks):
        first = other * BX - REACH - (brick * BX - H + off_ref[brick])
        moved = pltpu.roll(values, lax.rem(64 * tile_len - first, tile_len), 1)
        for j in range(parts):
            low = pltpu.roll(moved[:rows], (tile_len - SLAB * j) % tile_len, 1)[:, :128]
            high = pltpu.roll(moved[rows:], (tile_len + 64 - SLAB * j) % tile_len, 1)[:, :128]
            out_ref[j * bricks + other] = jnp.where(lane < 64, low, high).astype(BF)


def unpack_kernel(pieces_ref, out_ref):
    out_ref[...] = pieces_ref[...].reshape(128, 128).T[: out_ref.shape[0]]


def blended_slab(off_ref, ramp_ref, pieces_ref, first_col, total_cols, depth_parts, row_parts):
    bricks = lax.axis_size("gx")
    brick = lax.axis_index("gx")
    lane = lax.broadcasted_iota(jnp.int32, (1, 128), 1) % 64
    col = lane + (first_col - REACH)
    numerator = jnp.zeros((depth_parts, row_parts, 32, 128), F32)
    denominator = jnp.zeros((1, 128), F32)
    for step in range(min(bricks, 3)):
        if bricks > 3:
            tile = jnp.clip(brick - 1 + step, 0, bricks - 1)
            real = (brick - 1 + step >= 0) & (brick - 1 + step < bricks)
        else:
            tile, real = step, True
        tile_len = 2 * BX
        spot = col - (tile * BX - H + off_ref[tile])
        inside = (spot >= 0) & (spot < tile_len) & real
        width = ramp_ref[tile].astype(F32)
        spot = spot.astype(F32)
        weight = jnp.minimum(1.0, jnp.minimum((spot + 1.0) / width, (tile_len - spot) / width))
        weight = jnp.where(inside, weight, 0.0)
        denominator = denominator + weight
        values = pieces_ref[:, :, tile].astype(F32)
        numerator = numerator + values * weight
    good = (col >= 0) & (col < total_cols)
    result = jnp.where(good, numerator / jnp.where(good, denominator, 1.0), 0.0)
    zrows = result.reshape(depth_parts, row_parts, 4, 8, 128)
    low = zrows.transpose(0, 2, 1, 3, 4)
    high = pltpu.roll(result.reshape(-1, 128), 64, 1).reshape(zrows.shape).transpose(0, 2, 1, 3, 4)
    image = jnp.stack([low, high], axis=1).reshape(NZ * NY, 128)
    lanes = lax.broadcasted_iota(jnp.int32, image.shape, 1)
    return jnp.where(lanes < WIDE, image, 0.0)


def shifted(value, by):
    rows = value.shape[0]
    spot = lax.broadcasted_iota(jnp.int32, value.shape, 0) % NY
    moved = pltpu.roll(value, by % rows, 0)
    keep = (spot >= by) if by > 0 else (spot < NY + by)
    return jnp.where(keep, moved, 0.0)


def conv_kernel(
    off_ref, ramp_ref, pieces_ref, rows_ref, ws_ref, w0, w1, w2, w3, out_ref, stem_in, *acts
):
    w_refs = (w0, w1, w2, w3)
    depth_parts, row_parts = lax.axis_size("gz"), lax.axis_size("gy")
    slab = lax.axis_index("gz") * row_parts + lax.axis_index("gy")
    first_col = lax.axis_index("gx") * BX + slab * SLAB
    total_cols = lax.axis_size("gx") * BX

    def col_mask(layer, group, width):
        lane = lax.broadcasted_iota(jnp.int32, (1, width * C), 1) // C
        col = lane + (4 * group + first_col + ORIGIN[layer])
        return jnp.where((col >= 0) & (col < total_cols), 1.0, 0.0)

    for layer in range(LAYERS):
        spacing = 2**layer
        pad = jnp.zeros((3, spacing, NY, 4 * C), BF)
        for g in range(GROUPS[layer]):
            acts[layer][:, g, 1, :, 0] = pad
            acts[layer][:, g, 0, :, NZ // (2 * spacing) + 1] = pad

    image = blended_slab(
        off_ref, ramp_ref, pieces_ref, first_col, total_cols, depth_parts, row_parts
    )
    packed = shifted(image, 1)
    packed = packed + pltpu.roll(image, WIDE, 1)
    packed = packed + pltpu.roll(shifted(image, -1), 2 * WIDE, 1)
    coarse = packed.astype(BF)
    fine = (packed - coarse.astype(F32)).astype(BF)
    for part, value in enumerate((coarse, fine)):
        stem_in[part, 0] = jnp.zeros((NY, 128), BF)
        stem_in[part, NZ + 1] = jnp.zeros((NY, 128), BF)
        stem_in[part, 1 : NZ + 1] = value.reshape(NZ, NY, 128)

    def store(layer, group, plane_sets):
        spacing = 2**layer
        for lead, value in plane_sets:
            for s in range(3):
                part = value if s == 1 else shifted(value, spacing if s == 0 else -spacing)
                planes = part.astype(BF).reshape(lead[1], NZ // (2 * spacing), 2, NY, 4 * C)
                for b in range(2):
                    acts[layer][
                        s, group, b, lead[0] : lead[0] + lead[1], 1 : 1 + NZ // (2 * spacing)
                    ] = planes[:, :, b]

    def stem_tile(k, carry):
        acc = jnp.zeros((NZ * NY, 8 * C), F32)
        lhs = jnp.concatenate(
            [stem_in[p, c : c + NZ].reshape(NZ * NY, 128) for p in range(2) for c in range(3)],
            axis=1,
        )
        weights = jnp.concatenate([ws_ref[k], ws_ref[k]], axis=0)
        acc = jnp.dot(lhs, weights, preferred_element_type=F32)
        acc = jnp.maximum(acc + rows_ref[0:1], 0.0) * col_mask(0, 2 * k, 8)
        store(0, 2 * k, [((0, 1), acc[:, : 4 * C])])
        store(0, 2 * k + 1, [((0, 1), acc[:, 4 * C :])])
        return carry

    lax.fori_loop(0, GROUPS[0] // 2, stem_tile, 0)

    for layer in range(LAYERS):
        spacing = 2**layer
        count = NZ // (2 * spacing)
        src = acts[layer]

        def conv_group(g, carry, layer=layer, spacing=spacing, count=count, src=src):
            pieces = []
            for s in range(3):
                for i in range(TAPS[layer]):
                    for t in range(4):
                        piece = src[
                            s,
                            g + STEP[layer] * i,
                            1 - t % 2,
                            :,
                            (t + 1) // 2 : (t + 1) // 2 + count,
                        ]
                        pieces.append(piece.reshape(NZ * NY // 2, 4 * C))
            lhs = jnp.concatenate(pieces, axis=1)
            weights = w_refs[layer][...].reshape(3 * TAPS[layer] * 4 * 128, 8 * C)
            acc = jnp.dot(lhs, weights, preferred_element_type=F32)
            mask = col_mask(layer + 1, g, 4)
            halves = []
            for b in range(2):
                if layer < 2:
                    pair = jnp.concatenate(
                        [
                            src[1, g + i, b, :, 1 : 1 + count].reshape(NZ * NY // 2, 4 * C)
                            for i in range(2)
                        ],
                        axis=1,
                    ).astype(F32)
                    centre = pair[:, spacing * C : spacing * C + 4 * C]
                else:
                    centre = src[1, g + STEP[layer], b, :, 1 : 1 + count]
                    centre = centre.reshape(NZ * NY // 2, 4 * C).astype(F32)
                half = acc[:, 4 * C * b : 4 * C * (b + 1)] + rows_ref[8 + layer : 9 + layer, : 4 * C]
                halves.append(centre + jnp.maximum(half, 0.0) * mask)
            if layer + 1 < LAYERS:
                store(layer + 1, g, [((spacing * b, spacing), halves[b]) for b in range(2)])
            else:
                last = jnp.concatenate(halves, axis=1)
                last = last.reshape(spacing, count, row_parts, NY // row_parts, 8 * C)
                last = last.transpose(1, 2, 0, 3, 4).reshape(NZ * NY // 2, 8 * C).astype(BF)
                heads = lax.dot_general(
                    rows_ref[16:24].astype(BF),
                    last,
                    (((1,), (1,)), ((), ())),
                    preferred_element_type=F32,
                )
                size = NZ * NY // 2 // (count * row_parts)
                for m in range(count):
                    for y in range(row_parts):
                        at = (m * row_parts + y) * size
                        for b in range(2):
                            out_ref[
                                (2 * m + b) * row_parts + y, pl.ds(4 * g, 4), 0:size
                            ] = heads[4 * b : 4 * b + 4, at : at + size]
            return carry

        if layer + 1 < LAYERS:
            lax.fori_loop(0, GROUPS[layer + 1], conv_group, 0)
        else:
            for g in range(GROUPS[layer + 1]):
                conv_group(g, 0)


def vmem():
    return pl.BlockSpec(memory_space=pltpu.VMEM)


def body(
    stacks, offsets, ramp_width, stem_weight, stem_bias, layer_weight, layer_bias, head_weight
):
    depth_b, rows_b, tile_len = stacks.shape
    depth_parts, row_parts = lax.axis_size("gz"), lax.axis_size("gy")
    parts = depth_parts * row_parts
    bricks = lax.axis_size("gx")
    assert (depth_b * depth_parts, rows_b * row_parts, parts * SLAB) == (NZ, NY, BX)
    half = depth_b * rows_b // 2
    smem = pl.BlockSpec(memory_space=pltpu.SMEM)
    pieces = pl.pallas_call(
        functools.partial(pack_kernel, parts=parts, bricks=bricks),
        out_shape=jax.ShapeDtypeStruct((parts * bricks, half, 128), BF),
        in_specs=[smem, vmem()],
        out_specs=vmem(),
    )(offsets, stacks)
    pieces = lax.all_to_all(pieces, ("gz", "gy", "gx"), 0, 0, tiled=True)
    pieces = pieces.reshape(depth_parts, row_parts, bricks, half, 128)

    shapes = [
        jax.ShapeDtypeStruct((24, 8 * C), F32),
        jax.ShapeDtypeStruct((GROUPS[0] // 2, 384, 8 * C), BF),
    ] + [
        jax.ShapeDtypeStruct((3, TAPS[layer], 4, 4 * C, 8 * C), BF) for layer in range(LAYERS)
    ]
    weights = pl.pallas_call(
        weights_kernel,
        out_shape=shapes,
        in_specs=[vmem()] * 5,
        out_specs=[vmem()] * 6,
        scratch_shapes=[pltpu.VMEM((27, C, 4 * C), F32)],
        compiler_params=pltpu.CompilerParams(vmem_limit_bytes=32 * 2**20),
        cost_estimate=pl.CostEstimate(flops=4000000, bytes_accessed=9000000, transcendentals=0),
    )(layer_weight, layer_bias, stem_weight, stem_bias[None], head_weight[None])

    scratch = [pltpu.VMEM((2, NZ + 2, NY, 128), BF)] + [
        pltpu.VMEM((3, GROUPS[layer], 2, 2**layer, NZ // 2 ** (layer + 1) + 2, NY, 4 * C), BF)
        for layer in range(LAYERS)
    ]
    logits = pl.pallas_call(
        conv_kernel,
        out_shape=jax.ShapeDtypeStruct((parts, SLAB, 128), F32),
        in_specs=[smem, smem] + [vmem()] * 7,
        out_specs=vmem(),
        scratch_shapes=scratch,
        compiler_params=pltpu.CompilerParams(vmem_limit_bytes=60 * 2**20),
        cost_estimate=pl.CostEstimate(
            flops=20000000000, bytes_accessed=9000000, transcendentals=0
        ),
    )(offsets, ramp_width, pieces, *weights)
    logits = lax.all_to_all(logits, ("gz", "gy"), 0, 0, tiled=True)
    logits = pl.pallas_call(
        unpack_kernel,
        out_shape=jax.ShapeDtypeStruct((depth_b * rows_b, BX), F32),
        in_specs=[vmem()],
        out_specs=vmem(),
    )(logits)
    return logits.reshape(depth_b, rows_b, BX)


def solution(mesh):
    return jax.shard_map(
        body,
        mesh=mesh,
        in_specs=(P("gz", "gy", "gx"), P(), P(), P(), P(), P(), P(), P()),
        out_specs=P("gz", "gy", "gx"),
        check_vma=False,
    )
```

```python
import functools
import math

import jax
import jax.numpy as jnp
from jax import lax
from jax.experimental import pallas as pl
from jax.experimental.pallas import tpu as pltpu
from jax.sharding import PartitionSpec as P

LAYERS = 4
H = 64
S = 32
BX = 128
C = 32
REACH = 16
SLAB = 8
WIDE = SLAB + 2 * REACH
NZ = 32
NY = 32
GROUPS = (10, 9, 8, 6, 2)
TAPS = (2, 2, 3, 3)
STEP = (1, 1, 1, 2)
ORIGIN = (-15, -14, -12, -8, 0)
BF = jnp.bfloat16
F32 = jnp.float32


def repeated(row, copies):
    return jnp.concatenate([row] * copies, axis=1)


def weights_kernel(*refs):
    sources, rows_ref, outs, refs = refs[:5], refs[5], refs[6:11], refs[11:]
    inputs, built, turned, in_sems, out_sems = refs[:5], refs[5:10], *refs[10:]
    fetches = [
        pltpu.make_async_copy(a, b, in_sems.at[k]) for k, (a, b) in enumerate(zip(sources, inputs))
    ]
    stores = [
        pltpu.make_async_copy(a, b, out_sems.at[k]) for k, (a, b) in enumerate(zip(built, outs))
    ]
    for copy in fetches:
        copy.start()
    for copy in fetches:
        copy.wait()
    lw_ref, lb_ref, sw_ref, sb_ref, head_ref = inputs
    ws_ref, w_refs = built[0], built[1:]
    lane = lax.broadcasted_iota(jnp.int32, (C, 4 * C), 1) // C
    zero = jnp.zeros((C, 4 * C), BF)
    for layer in range(LAYERS):
        spacing = 2**layer
        out = w_refs[layer]
        flat = lw_ref[layer].astype(F32).reshape(27 * C, C)
        flat = jnp.concatenate([flat, jnp.zeros((28 * 4 * C - 27 * C, C), F32)], axis=0)
        flat = jnp.concatenate([flat, jnp.zeros((28 * 4 * C, 3 * C), F32)], axis=1)
        for t in range(27):
            turned[t] = flat[C * t : C * t + 4 * C].T[:C]

        def per_row_tap(s, carry, layer=layer, spacing=spacing, out=out):
            taps = []
            for c in range(3):
                taps.append([])
                for a in range(3):
                    block = jnp.where(lane == 0, turned[9 * c + a + 3 * s], 0.0)
                    block = block + pltpu.roll(block, 2 * C, 1)
                    taps[c].append(block + pltpu.roll(block, C, 1))
            for i in range(TAPS[layer]):
                for xi in range(4):
                    rows = pl.ds(xi * C, C)
                    for c in range(3):
                        block = jnp.zeros((C, 4 * C), F32)
                        for a in range(3):
                            xo = 4 * STEP[layer] * i + xi - spacing * a
                            if 0 <= xo < 4:
                                block = jnp.where(lane == xo, taps[c][a], block)
                        block = block.astype(BF)
                        out[s, i, c, rows, 0 : 4 * C] = block
                        out[s, i, c + 1, rows, 4 * C : 8 * C] = block
                    out[s, i, 0, rows, 4 * C : 8 * C] = zero
                    out[s, i, 3, rows, 0 : 4 * C] = zero
            return carry

        lax.fori_loop(0, 3, per_row_tap, 0)
        stores[1 + layer].start()
    row = lax.broadcasted_iota(jnp.int32, (128, 8 * C), 0)
    column = lax.broadcasted_iota(jnp.int32, (128, 8 * C), 1) // C
    stem = repeated(sw_ref[...].astype(F32), 8)

    def per_tile(k, carry):
        diff = row - column - 8 * k
        for c in range(3):
            block = jnp.zeros((128, 8 * C), F32)
            for b in range(3):
                for a in range(3):
                    tap = 9 * c + 3 * b + a
                    block = jnp.where(diff == WIDE * b + a, stem[tap : tap + 1, :], block)
            ws_ref[k, 128 * c : 128 * (c + 1), :] = block.astype(BF)
        return carry

    lax.fori_loop(0, GROUPS[0] // 2, per_tile, 0)
    stores[0].start()
    rows_ref[...] = jnp.zeros(rows_ref.shape, F32)
    rows_ref[0:1, :] = repeated(sb_ref[...], 8)
    for layer in range(LAYERS):
        rows_ref[8 + layer : 9 + layer, :] = repeated(lb_ref[layer : layer + 1], 8)
    head = repeated(head_ref[...].astype(F32), 8)
    spot = lax.broadcasted_iota(jnp.int32, (8, 8 * C), 0)
    rows_ref[16:24, :] = jnp.where(spot == column[:8], head, 0.0)
    for copy in stores:
        copy.wait()


def pack_kernel(off_ref, stacks_ref, out_ref, *, parts, bricks):
    brick = lax.axis_index("gx")
    tile_len = stacks_ref.shape[2]
    rows = out_ref.shape[1]
    values = stacks_ref[...].astype(F32).reshape(2 * rows, tile_len)
    lane = lax.broadcasted_iota(jnp.int32, (rows, 128), 1)
    for other in range(bricks):
        first = other * BX - REACH - (brick * BX - H + off_ref[brick])
        moved = pltpu.roll(values, lax.rem(64 * tile_len - first, tile_len), 1)
        for j in range(parts):
            low = pltpu.roll(moved[:rows], (tile_len - SLAB * j) % tile_len, 1)[:, :128]
            high = pltpu.roll(moved[rows:], (tile_len + 64 - SLAB * j) % tile_len, 1)[:, :128]
            out_ref[j * bricks + other] = jnp.where(lane < 64, low, high).astype(BF)


def unpack_kernel(pieces_ref, out_ref):
    out_ref[...] = pieces_ref[...].reshape(128, 128).T[: out_ref.shape[0]]


def blended_slab(off_ref, ramp_ref, pieces_ref, first_col, total_cols, depth_parts, row_parts):
    bricks = lax.axis_size("gx")
    brick = lax.axis_index("gx")
    lane = lax.broadcasted_iota(jnp.int32, (1, 128), 1) % 64
    col = lane + (first_col - REACH)
    numerator = jnp.zeros((depth_parts, row_parts, 32, 128), F32)
    denominator = jnp.zeros((1, 128), F32)
    for step in range(min(bricks, 3)):
        if bricks > 3:
            tile = jnp.clip(brick - 1 + step, 0, bricks - 1)
            real = (brick - 1 + step >= 0) & (brick - 1 + step < bricks)
        else:
            tile, real = step, True
        tile_len = 2 * BX
        spot = col - (tile * BX - H + off_ref[tile])
        inside = (spot >= 0) & (spot < tile_len) & real
        width = ramp_ref[tile].astype(F32)
        spot = spot.astype(F32)
        weight = jnp.minimum(1.0, jnp.minimum((spot + 1.0) / width, (tile_len - spot) / width))
        weight = jnp.where(inside, weight, 0.0)
        denominator = denominator + weight
        values = pieces_ref[:, :, tile].astype(F32)
        numerator = numerator + values * weight
    good = (col >= 0) & (col < total_cols)
    result = jnp.where(good, numerator / jnp.where(good, denominator, 1.0), 0.0)
    zrows = result.reshape(depth_parts, row_parts, 4, 8, 128)
    low = zrows.transpose(0, 2, 1, 3, 4)
    high = pltpu.roll(result.reshape(-1, 128), 64, 1).reshape(zrows.shape).transpose(0, 2, 1, 3, 4)
    image = jnp.stack([low, high], axis=1).reshape(NZ * NY, 128)
    lanes = lax.broadcasted_iota(jnp.int32, image.shape, 1)
    return jnp.where(lanes < WIDE, image, 0.0)


def shifted(value, by):
    rows = value.shape[0]
    spot = lax.broadcasted_iota(jnp.int32, value.shape, 0) % NY
    moved = pltpu.roll(value, by % rows, 0)
    keep = (spot >= by) if by > 0 else (spot < NY + by)
    return jnp.where(keep, moved, 0.0)


def act_shape(layer):
    return (3, GROUPS[layer], 2, 2**layer, NZ // 2 ** (layer + 1) + 2, NY, 4 * C)


def act_rows(layer):
    return math.prod(act_shape(layer)[:-2])


def conv_kernel(off_ref, ramp_ref, pieces_ref, rows_ref, *refs):
    built, out_ref, refs = refs[:5], refs[5], refs[6:]
    held, stem_in, spaces, accs, sems = refs[:5], refs[5], refs[6:8], refs[8:10], refs[10]
    fetches = [
        pltpu.make_async_copy(a, b, sems.at[k]) for k, (a, b) in enumerate(zip(built, held))
    ]
    for copy in fetches:
        copy.start()
    ws_ref, w_refs = held[0], held[1:]
    acts = [
        spaces[layer % 2].at[0 : act_rows(layer)].reshape(act_shape(layer))
        for layer in range(LAYERS)
    ]
    depth_parts, row_parts = lax.axis_size("gz"), lax.axis_size("gy")
    slab = lax.axis_index("gz") * row_parts + lax.axis_index("gy")
    first_col = lax.axis_index("gx") * BX + slab * SLAB
    total_cols = lax.axis_size("gx") * BX

    def col_mask(layer, group, width):
        lane = lax.broadcasted_iota(jnp.int32, (1, width * C), 1) // C
        col = lane + (4 * group + first_col + ORIGIN[layer])
        return jnp.where((col >= 0) & (col < total_cols), 1.0, 0.0)

    def clear_edges(layer):
        spacing = 2**layer
        pad = jnp.zeros((3, spacing, NY, 4 * C), BF)
        for g in range(GROUPS[layer]):
            acts[layer][:, g, 1, :, 0] = pad
            acts[layer][:, g, 0, :, NZ // (2 * spacing) + 1] = pad

    def store(layer, group, start, length, value):
        spacing = 2**layer
        for s in range(3):
            part = value if s == 1 else shifted(value, spacing if s == 0 else -spacing)
            planes = part.astype(BF).reshape(length, -1, 2, NY, 4 * C)
            for b in range(2):
                acts[layer][s, group, b, start : start + length, 1 : 1 + planes.shape[1]] = planes[
                    :, :, b
                ]

    def store_plane(layer, group, start, length, m, value):
        spacing = 2**layer
        for s in range(3):
            part = value if s == 1 else shifted(value, spacing if s == 0 else -spacing)
            planes = part.astype(BF).reshape(length, NY, 4 * C)
            acts[layer][s, group, m % 2, start : start + length, 1 + m // 2] = planes

    clear_edges(0)
    image = blended_slab(
        off_ref, ramp_ref, pieces_ref, first_col, total_cols, depth_parts, row_parts
    )
    packed = shifted(image, 1)
    packed = packed + pltpu.roll(image, WIDE, 1)
    packed = packed + pltpu.roll(shifted(image, -1), 2 * WIDE, 1)
    coarse = packed.astype(BF)
    fine = (packed - coarse.astype(F32)).astype(BF)
    for part, value in enumerate((coarse, fine)):
        stem_in[part, 0] = jnp.zeros((NY, 128), BF)
        stem_in[part, NZ + 1] = jnp.zeros((NY, 128), BF)
        stem_in[part, 1 : NZ + 1] = value.reshape(NZ, NY, 128)

    def stem_dot(k):
        lhs = jnp.concatenate(
            [stem_in[p, c : c + NZ].reshape(NZ * NY, 128) for p in range(2) for c in range(3)],
            axis=1,
        )
        weights = jnp.concatenate([ws_ref[k], ws_ref[k]], axis=0)
        return jnp.dot(lhs, weights, preferred_element_type=F32)

    def stem_finish(k, acc):
        value = jnp.maximum(acc + rows_ref[0:1], 0.0) * col_mask(0, 2 * k, 8)
        store(0, 2 * k, 0, 1, value[:, : 4 * C])
        store(0, 2 * k + 1, 0, 1, value[:, 4 * C :])

    def group_dot(layer, g):
        spacing = 2**layer
        count = NZ // (2 * spacing)
        pieces = []
        for s in range(3):
            for i in range(TAPS[layer]):
                for t in range(4):
                    start = (t + 1) // 2
                    piece = acts[layer][s, g + i, 1 - t % 2, :, start : start + count]
                    pieces.append(piece.reshape(NZ * NY // 2, 4 * C))
        lhs = jnp.concatenate(pieces, axis=1)
        weights = w_refs[layer][...].reshape(12 * TAPS[layer] * 4 * C, 8 * C)
        return jnp.dot(lhs, weights, preferred_element_type=F32)

    def group_finish(layer, g, acc):
        spacing = 2**layer
        count = NZ // (2 * spacing)
        mask = col_mask(layer + 1, g, 4)
        bias = rows_ref[8 + layer : 9 + layer, : 4 * C]
        for b in range(2):
            pair = jnp.concatenate(
                [
                    acts[layer][1, g + i, b, :, 1 : 1 + count].reshape(NZ * NY // 2, 4 * C)
                    for i in range(2)
                ],
                axis=1,
            ).astype(F32)
            centre = pair[:, spacing * C : spacing * C + 4 * C]
            half = acc[0 : NZ * NY // 2, 4 * C * b : 4 * C * (b + 1)] + bias
            value = centre + jnp.maximum(half, 0.0) * mask
            store(layer + 1, g, spacing * b, spacing, value)

    def plane_dot(layer, m):
        spacing = 2**layer
        groups = GROUPS[layer + 1]
        taps = [t for t in range(4) if 0 < m + (t + 1) // 2 < NZ // (2 * spacing) + 1]
        pieces, weights = [], []
        for s in range(3):
            for i in range(TAPS[layer]):
                for t in taps:
                    first = STEP[layer] * i
                    piece = acts[layer][s, first : first + groups, 1 - t % 2, :, m + (t + 1) // 2]
                    pieces.append(piece.reshape(groups * spacing * NY, 4 * C))
                    weights.append(w_refs[layer][s, i, t])
        return jnp.dot(
            jnp.concatenate(pieces, axis=1),
            jnp.concatenate(weights, axis=0),
            preferred_element_type=F32,
        )

    def plane_values(layer, m, g, acc):
        spacing = 2**layer
        rows = spacing * NY
        mask = col_mask(layer + 1, g, 4)
        bias = rows_ref[8 + layer : 9 + layer, : 4 * C]
        values = []
        for b in range(2):
            centre = acts[layer][1, g + STEP[layer], b, :, 1 + m].reshape(rows, 4 * C)
            half = acc[g * rows : (g + 1) * rows, 4 * C * b : 4 * C * (b + 1)] + bias
            values.append(centre.astype(F32) + jnp.maximum(half, 0.0) * mask)
        return values

    def plane_finish(layer, m, acc):
        spacing = 2**layer
        for g in range(GROUPS[layer + 1]):
            for b, value in enumerate(plane_values(layer, m, g, acc)):
                store_plane(layer + 1, g, spacing * b, spacing, m, value)

    def head_finish(m, acc):
        layer = LAYERS - 1
        spacing = 2**layer
        for g in range(GROUPS[layer + 1]):
            last = jnp.concatenate(plane_values(layer, m, g, acc), axis=1)
            last = last.reshape(spacing, row_parts, NY // row_parts, 8 * C)
            last = last.transpose(1, 0, 2, 3).reshape(spacing * NY, 8 * C).astype(BF)
            heads = lax.dot_general(
                rows_ref[16:24].astype(BF),
                last,
                (((1,), (1,)), ((), ())),
                preferred_element_type=F32,
            )
            size = spacing * NY // row_parts
            for y in range(row_parts):
                for b in range(2):
                    out_ref[(2 * m + b) * row_parts + y, 4 * g : 4 * g + 4, 0:size] = heads[
                        4 * b : 4 * b + 4, y * size : (y + 1) * size
                    ]

    def in_line(count, dot, finish):
        for k in range(count):
            finish(k, dot(k))

    fetches[0].wait()
    in_line(GROUPS[0] // 2, stem_dot, stem_finish)
    for layer in range(LAYERS):
        fetches[1 + layer].wait()
        if layer + 1 < LAYERS:
            clear_edges(layer + 1)
        if layer < 2:
            in_line(
                GROUPS[layer + 1],
                functools.partial(group_dot, layer),
                functools.partial(group_finish, layer),
            )
        elif layer + 1 < LAYERS:
            in_line(
                NZ // 2 ** (layer + 1),
                functools.partial(plane_dot, layer),
                functools.partial(plane_finish, layer),
            )
        else:
            for m in range(NZ // 2 ** (layer + 1)):
                accs[m][...] = plane_dot(layer, m)
                if m:
                    head_finish(m - 1, accs[m - 1])
            head_finish(m, accs[m])


def vmem():
    return pl.BlockSpec(memory_space=pltpu.VMEM)


def body(
    stacks, offsets, ramp_width, stem_weight, stem_bias, layer_weight, layer_bias, head_weight
):
    depth_b, rows_b, tile_len = stacks.shape
    depth_parts, row_parts = lax.axis_size("gz"), lax.axis_size("gy")
    parts = depth_parts * row_parts
    bricks = lax.axis_size("gx")
    assert (depth_b * depth_parts, rows_b * row_parts, parts * SLAB) == (NZ, NY, BX)
    half = depth_b * rows_b // 2
    smem = pl.BlockSpec(memory_space=pltpu.SMEM)
    pieces = pl.pallas_call(
        functools.partial(pack_kernel, parts=parts, bricks=bricks),
        out_shape=jax.ShapeDtypeStruct((parts * bricks, half, 128), BF),
        in_specs=[smem, vmem()],
        out_specs=vmem(),
    )(offsets, stacks)
    pieces = lax.all_to_all(pieces, ("gz", "gy", "gx"), 0, 0, tiled=True)
    pieces = pieces.reshape(depth_parts, row_parts, bricks, half, 128)

    hbm = pl.BlockSpec(memory_space=pltpu.HBM)
    small = jax.ShapeDtypeStruct((24, 8 * C), F32)
    shapes = [jax.ShapeDtypeStruct((GROUPS[0] // 2, 384, 8 * C), BF)] + [
        jax.ShapeDtypeStruct((3, TAPS[layer], 4, 4 * C, 8 * C), BF) for layer in range(LAYERS)
    ]
    spaces = [pltpu.VMEM(shape.shape, shape.dtype) for shape in shapes]
    raw = (layer_weight, layer_bias, stem_weight, stem_bias[None], head_weight[None])
    rows, *weights = pl.pallas_call(
        weights_kernel,
        out_shape=[small] + shapes,
        in_specs=[hbm] * 5,
        out_specs=[vmem()] + [hbm] * 5,
        scratch_shapes=[pltpu.VMEM(array.shape, array.dtype) for array in raw]
        + spaces
        + [
            pltpu.VMEM((27, C, 4 * C), F32),
            pltpu.SemaphoreType.DMA((5,)),
            pltpu.SemaphoreType.DMA((5,)),
        ],
        compiler_params=pltpu.CompilerParams(vmem_limit_bytes=64 * 2**20 - 2**18),
        cost_estimate=pl.CostEstimate(flops=4000000, bytes_accessed=9000000, transcendentals=0),
    )(*raw)

    held = [max(act_rows(layer) for layer in range(odd, LAYERS, 2)) for odd in range(2)]
    scratch = (
        spaces
        + [pltpu.VMEM((2, NZ + 2, NY, 128), BF)]
        + [pltpu.VMEM((size, NY, 4 * C), BF) for size in held]
        + [pltpu.VMEM((NZ * NY // 2, 8 * C), F32)] * 2
        + [pltpu.SemaphoreType.DMA((5,))]
    )
    logits = pl.pallas_call(
        conv_kernel,
        out_shape=jax.ShapeDtypeStruct((parts, SLAB, 128), F32),
        in_specs=[smem, smem, vmem(), vmem()] + [hbm] * 5,
        out_specs=vmem(),
        scratch_shapes=scratch,
        compiler_params=pltpu.CompilerParams(vmem_limit_bytes=64 * 2**20 - 2**18),
        cost_estimate=pl.CostEstimate(
            flops=20000000000, bytes_accessed=9000000, transcendentals=0
        ),
    )(offsets, ramp_width, pieces, rows, *weights)
    logits = lax.all_to_all(logits, ("gz", "gy"), 0, 0, tiled=True)
    logits = pl.pallas_call(
        unpack_kernel,
        out_shape=jax.ShapeDtypeStruct((depth_b * rows_b, BX), F32),
        in_specs=[vmem()],
        out_specs=vmem(),
    )(logits)
    return logits.reshape(depth_b, rows_b, BX)


def solution(mesh):
    return jax.shard_map(
        body,
        mesh=mesh,
        in_specs=(P("gz", "gy", "gx"), P(), P(), P(), P(), P(), P(), P()),
        out_specs=P("gz", "gy", "gx"),
        check_vma=False,
    )
```

```python
import functools
import math

import jax
import jax.numpy as jnp
from jax import lax
from jax.experimental import pallas as pl
from jax.experimental.pallas import tpu as pltpu
from jax.sharding import PartitionSpec as P

LAYERS = 4
H = 64
S = 32
BX = 128
C = 32
REACH = 16
SLAB = 8
WIDE = SLAB + 2 * REACH
NZ = 32
NY = 32
GROUPS = (10, 5, 4, 3, 1)
PHASES = (1, 2, 2, 2, 2)
TAPS = (2, 2, 2, 3)
COLSTEP = (1, 1, 2, 4)
PACKED = 2
ORIGIN = (-15, -14, -12, -8, 0)
BF = jnp.bfloat16
F32 = jnp.float32


def repeated(row, copies):
    return jnp.concatenate([row] * copies, axis=1)


def weights_kernel(*refs):
    sources, rows_ref, outs, refs = refs[:5], refs[5], refs[6:11], refs[11:]
    inputs, built, turned, in_sems, out_sems = refs[:5], refs[5:10], *refs[10:]
    fetches = [
        pltpu.make_async_copy(a, b, in_sems.at[k]) for k, (a, b) in enumerate(zip(sources, inputs))
    ]
    stores = [
        pltpu.make_async_copy(a, b, out_sems.at[k]) for k, (a, b) in enumerate(zip(built, outs))
    ]
    for copy in fetches:
        copy.start()
    for copy in fetches:
        copy.wait()
    lw_ref, lb_ref, sw_ref, sb_ref, head_ref = inputs
    ws_ref, w_refs = built[0], built[1:]
    lane = lax.broadcasted_iota(jnp.int32, (C, 4 * C), 1) // C
    zero = jnp.zeros((C, 4 * C), BF)
    for layer in range(LAYERS):
        spacing = 2**layer
        out = w_refs[layer]
        flat = lw_ref[layer].astype(F32).reshape(27 * C, C)
        flat = jnp.concatenate([flat, jnp.zeros((28 * 4 * C - 27 * C, C), F32)], axis=0)
        flat = jnp.concatenate([flat, jnp.zeros((28 * 4 * C, 3 * C), F32)], axis=1)
        for t in range(27):
            turned[t] = flat[C * t : C * t + 4 * C].T[:C]

        def per_row_tap(s, carry, layer=layer, spacing=spacing, out=out):
            taps = []
            for c in range(3):
                taps.append([])
                for a in range(3):
                    block = jnp.where(lane == 0, turned[9 * c + a + 3 * s], 0.0)
                    block = block + pltpu.roll(block, 2 * C, 1)
                    taps[c].append(block + pltpu.roll(block, C, 1))
            def place(i, t, xi, b, block):
                lanes = slice(4 * C * b, 4 * C * (b + 1))
                if layer >= PACKED:
                    out[s, i, t, xi * C : (xi + 1) * C, lanes] = block
                elif i == 0:
                    out[s, t, xi * C : (xi + 1) * C, lanes] = block
                else:
                    first = 2 * C * (t % 2) + xi * C
                    out[s, 4 + t // 2, first : first + C, lanes] = block

            for i in range(TAPS[layer]):
                for xi in range(4 if i == 0 or layer >= PACKED else 2):
                    for c in range(3):
                        block = jnp.zeros((C, 4 * C), F32)
                        for a in range(3):
                            xo = 4 * i + xi - COLSTEP[layer] * a
                            if 0 <= xo < 4:
                                block = jnp.where(lane == xo, taps[c][a], block)
                        block = block.astype(BF)
                        for b in range(2):
                            place(i, c + b, xi, b, block)
                    place(i, 0, xi, 1, zero)
                    place(i, 3, xi, 0, zero)
            return carry

        lax.fori_loop(0, 3, per_row_tap, 0)
        stores[1 + layer].start()
    row = lax.broadcasted_iota(jnp.int32, (128, 8 * C), 0)
    column = lax.broadcasted_iota(jnp.int32, (128, 8 * C), 1) // C
    stem = repeated(sw_ref[...].astype(F32), 8)

    def per_tile(k, carry):
        diff = row - column - 8 * k
        for c in range(3):
            block = jnp.zeros((128, 8 * C), F32)
            for b in range(3):
                for a in range(3):
                    tap = 9 * c + 3 * b + a
                    block = jnp.where(diff == WIDE * b + a, stem[tap : tap + 1, :], block)
            ws_ref[k, 128 * c : 128 * (c + 1), :] = block.astype(BF)
        return carry

    lax.fori_loop(0, GROUPS[0] // 2, per_tile, 0)
    stores[0].start()
    rows_ref[...] = jnp.zeros(rows_ref.shape, F32)
    rows_ref[0:1, :] = repeated(sb_ref[...], 8)
    for layer in range(LAYERS):
        rows_ref[8 + layer : 9 + layer, :] = repeated(lb_ref[layer : layer + 1], 8)
    head = repeated(head_ref[...].astype(F32), 8)
    spot = lax.broadcasted_iota(jnp.int32, (8, 8 * C), 0)
    rows_ref[16:24, :] = jnp.where(spot == column[:8], head, 0.0)
    for copy in stores:
        copy.wait()


def pack_kernel(off_ref, stacks_ref, out_ref, *, parts, bricks):
    brick = lax.axis_index("gx")
    tile_len = stacks_ref.shape[2]
    rows = out_ref.shape[1]
    values = stacks_ref[...].astype(F32).reshape(2 * rows, tile_len)
    lane = lax.broadcasted_iota(jnp.int32, (rows, 128), 1)
    for other in range(bricks):
        first = other * BX - REACH - (brick * BX - H + off_ref[brick])
        moved = pltpu.roll(values, lax.rem(64 * tile_len - first, tile_len), 1)
        for j in range(parts):
            low = pltpu.roll(moved[:rows], (tile_len - SLAB * j) % tile_len, 1)[:, :128]
            high = pltpu.roll(moved[rows:], (tile_len + 64 - SLAB * j) % tile_len, 1)[:, :128]
            out_ref[j * bricks + other] = jnp.where(lane < 64, low, high).astype(BF)


def unpack_kernel(pieces_ref, out_ref):
    out_ref[...] = pieces_ref[...].reshape(128, 128).T[: out_ref.shape[0]]


def blended_slab(off_ref, ramp_ref, pieces_ref, first_col, total_cols, depth_parts, row_parts):
    bricks = lax.axis_size("gx")
    brick = lax.axis_index("gx")
    lane = lax.broadcasted_iota(jnp.int32, (1, 128), 1) % 64
    col = lane + (first_col - REACH)
    numerator = jnp.zeros((depth_parts, row_parts, 32, 128), F32)
    denominator = jnp.zeros((1, 128), F32)
    for step in range(min(bricks, 3)):
        if bricks > 3:
            tile = jnp.clip(brick - 1 + step, 0, bricks - 1)
            real = (brick - 1 + step >= 0) & (brick - 1 + step < bricks)
        else:
            tile, real = step, True
        tile_len = 2 * BX
        spot = col - (tile * BX - H + off_ref[tile])
        inside = (spot >= 0) & (spot < tile_len) & real
        width = ramp_ref[tile].astype(F32)
        spot = spot.astype(F32)
        weight = jnp.minimum(1.0, jnp.minimum((spot + 1.0) / width, (tile_len - spot) / width))
        weight = jnp.where(inside, weight, 0.0)
        denominator = denominator + weight
        values = pieces_ref[:, :, tile].astype(F32)
        numerator = numerator + values * weight
    good = (col >= 0) & (col < total_cols)
    result = jnp.where(good, numerator / jnp.where(good, denominator, 1.0), 0.0)
    zrows = result.reshape(depth_parts, row_parts, 4, 8, 128)
    low = zrows.transpose(0, 2, 1, 3, 4)
    high = pltpu.roll(result.reshape(-1, 128), 64, 1).reshape(zrows.shape).transpose(0, 2, 1, 3, 4)
    image = jnp.stack([low, high], axis=1).reshape(NZ * NY, 128)
    lanes = lax.broadcasted_iota(jnp.int32, image.shape, 1)
    return jnp.where(lanes < WIDE, image, 0.0)


def shifted(value, by):
    rows = value.shape[0]
    spot = lax.broadcasted_iota(jnp.int32, value.shape, 0) % NY
    moved = pltpu.roll(value, by % rows, 0)
    keep = (spot >= by) if by > 0 else (spot < NY + by)
    return jnp.where(keep, moved, 0.0)


def weight_shape(layer):
    return (3, 6, 4 * C, 8 * C) if layer < PACKED else (3, TAPS[layer], 4, 4 * C, 8 * C)


def act_shape(layer):
    planes = NZ // 2 ** (layer + 1) + 2
    return (3, PHASES[layer], GROUPS[layer], 2, 2**layer, planes, NY, 4 * C)


def edge_shape(layer):
    planes = NZ // 2 ** (layer + 1) + 1
    return (3, PHASES[layer], GROUPS[layer] - 1, 2**layer, planes, NY, 4 * C)


def act_rows(layer):
    return math.prod(act_shape(layer)[:-2])


def conv_kernel(off_ref, ramp_ref, pieces_ref, rows_ref, *refs):
    built, out_ref, refs = refs[:5], refs[5], refs[6:]
    held, stem_in, spaces, accs = refs[:5], refs[5], refs[6:8], refs[8:10]
    sems, edges = refs[10], refs[11:]
    fetches = [
        pltpu.make_async_copy(a, b, sems.at[k]) for k, (a, b) in enumerate(zip(built, held))
    ]
    for copy in fetches:
        copy.start()
    ws_ref, w_refs = held[0], held[1:]
    acts = [
        spaces[layer % 2].at[0 : act_rows(layer)].reshape(act_shape(layer))
        for layer in range(LAYERS)
    ]
    depth_parts, row_parts = lax.axis_size("gz"), lax.axis_size("gy")
    slab = lax.axis_index("gz") * row_parts + lax.axis_index("gy")
    first_col = lax.axis_index("gx") * BX + slab * SLAB
    total_cols = lax.axis_size("gx") * BX

    def col_mask(start, step, width):
        lane = lax.broadcasted_iota(jnp.int32, (1, width * C), 1) // C
        col = step * lane + (first_col + start)
        return jnp.where((col >= 0) & (col < total_cols), 1.0, 0.0)

    def clear_edges(layer):
        spacing = 2**layer
        pad = jnp.zeros((3, spacing, NY, 4 * C), BF)
        for phase in range(PHASES[layer]):
            for g in range(GROUPS[layer]):
                acts[layer][:, phase, g, 1, :, 0] = pad
                acts[layer][:, phase, g, 0, :, NZ // (2 * spacing) + 1] = pad

    def store(layer, phase, group, start, length, value):
        spacing = 2**layer
        rows = slice(start, start + length)
        for s in range(3):
            part = value if s == 1 else shifted(value, spacing if s == 0 else -spacing)
            planes = part.astype(BF).reshape(length, -1, 2, NY, 4 * C)
            count = planes.shape[1]
            low, high = planes[:, :, 0], planes[:, :, 1]
            acts[layer][s, phase, group, 0, rows, 1 : 1 + count] = low
            acts[layer][s, phase, group, 1, rows, 1 : 1 + count] = high
            if layer < PACKED and group > 0:
                low, high = low[..., : 2 * C], high[..., : 2 * C]
                blank = jnp.zeros((length, 1, NY, 2 * C), BF)
                out = edges[layer]
                first = jnp.concatenate([blank, low[:, :1]], axis=-1)
                inner = jnp.concatenate([high[:, :-1], low[:, 1:]], axis=-1)
                last = jnp.concatenate([high[:, -1:], blank], axis=-1)
                out[s, phase, group - 1, rows, 0:1] = first
                out[s, phase, group - 1, rows, 1:count] = inner
                out[s, phase, group - 1, rows, count : count + 1] = last

    def store_plane(layer, phase, group, start, length, m, value):
        spacing = 2**layer
        for s in range(3):
            part = value if s == 1 else shifted(value, spacing if s == 0 else -spacing)
            planes = part.astype(BF).reshape(length, NY, 4 * C)
            acts[layer][s, phase, group, m % 2, start : start + length, 1 + m // 2] = planes

    clear_edges(0)
    image = blended_slab(
        off_ref, ramp_ref, pieces_ref, first_col, total_cols, depth_parts, row_parts
    )
    packed = shifted(image, 1)
    packed = packed + pltpu.roll(image, WIDE, 1)
    packed = packed + pltpu.roll(shifted(image, -1), 2 * WIDE, 1)
    coarse = packed.astype(BF)
    fine = (packed - coarse.astype(F32)).astype(BF)
    for part, value in enumerate((coarse, fine)):
        stem_in[part, 0] = jnp.zeros((NY, 128), BF)
        stem_in[part, NZ + 1] = jnp.zeros((NY, 128), BF)
        stem_in[part, 1 : NZ + 1] = value.reshape(NZ, NY, 128)

    def stem_dot(k):
        lhs = jnp.concatenate(
            [stem_in[p, c : c + NZ].reshape(NZ * NY, 128) for p in range(2) for c in range(3)],
            axis=1,
        )
        weights = jnp.concatenate([ws_ref[k], ws_ref[k]], axis=0)
        return jnp.dot(lhs, weights, preferred_element_type=F32)

    def stem_finish(k, acc):
        mask = col_mask(8 * k + ORIGIN[0], 1, 8)
        value = jnp.maximum(acc + rows_ref[0:1], 0.0) * mask
        store(0, 0, 2 * k, 0, 1, value[:, : 4 * C])
        store(0, 0, 2 * k + 1, 0, 1, value[:, 4 * C :])

    def group_dot(layer, phase, g):
        spacing = 2**layer
        count = NZ // (2 * spacing)
        rows = NZ * NY // 2
        pieces = []
        for s in range(3):
            for t in range(4):
                start = (t + 1) // 2
                piece = acts[layer][s, phase, g, 1 - t % 2, :, start : start + count]
                pieces.append(piece.reshape(rows, 4 * C))
            for start in range(2):
                piece = edges[layer][s, phase, g, :, start : start + count]
                pieces.append(piece.reshape(rows, 4 * C))
        lhs = jnp.concatenate(pieces, axis=1)
        weights = w_refs[layer][...].reshape(18 * 4 * C, 8 * C)
        return jnp.dot(lhs, weights, preferred_element_type=F32)

    def centred(layer, phase, g, b, planes, rows):
        near = [acts[layer][1, phase, g + i, b, :, planes].reshape(rows, 4 * C) for i in range(2)]
        pair = jnp.concatenate(near, axis=1).astype(F32)
        first = COLSTEP[layer] * C
        return pair[:, first : first + 4 * C]

    def group_values(layer, phase, g, acc, mask):
        count = NZ // (2 * 2**layer)
        bias = rows_ref[8 + layer : 9 + layer, : 4 * C]
        values = []
        for b in range(2):
            centre = centred(layer, phase, g, b, slice(1, 1 + count), NZ * NY // 2)
            half = acc[:, 4 * C * b : 4 * C * (b + 1)] + bias
            values.append(centre + jnp.maximum(half, 0.0) * mask)
        return values

    def split_store(k, left, right):
        for b in range(2):
            one = left[b]
            block = lax.broadcasted_iota(jnp.int32, one.shape, 1) // C
            up, far = pltpu.roll(one, 3 * C, 1), pltpu.roll(one, 2 * C, 1)
            even = jnp.where(block == 0, one, up)
            odd = jnp.where(block == 0, up, far)
            if right is None:
                even_end = odd_end = jnp.zeros_like(one)
            else:
                two = right[b]
                down, far = pltpu.roll(two, C, 1), pltpu.roll(two, 2 * C, 1)
                even_end = jnp.where(block == 2, far, down)
                odd_end = jnp.where(block == 2, down, two)
            store(1, 0, k, b, 1, jnp.where(block < 2, even, even_end))
            store(1, 1, k, b, 1, jnp.where(block < 2, odd, odd_end))

    def first_layer():
        left = None
        for g in range(GROUPS[0] - 1):
            mask = col_mask(4 * g + ORIGIN[1], 1, 4)
            values = group_values(0, 0, g, group_dot(0, 0, g), mask)
            if left is None:
                left = values
            else:
                split_store(g // 2, left, values)
                left = None
        split_store(GROUPS[1] - 1, left, None)

    def second_layer():
        for phase in range(2):
            for g in range(GROUPS[2]):
                mask = col_mask(8 * g + phase + ORIGIN[2], 2, 4)
                values = group_values(1, phase, g, group_dot(1, phase, g), mask)
                for b in range(2):
                    store(2, phase, g, 2 * b, 2, values[b])

    def plane_dot(layer, m):
        spacing = 2**layer
        groups = GROUPS[layer + 1]
        taps = [t for t in range(4) if 0 < m + (t + 1) // 2 < NZ // (2 * spacing) + 1]
        pieces, weights = [], []
        for s in range(3):
            for i in range(TAPS[layer]):
                for t in taps:
                    piece = acts[layer][s, :, i : i + groups, 1 - t % 2, :, m + (t + 1) // 2]
                    pieces.append(piece.reshape(2 * groups * spacing * NY, 4 * C))
                    weights.append(w_refs[layer][s, i, t])
        return jnp.dot(
            jnp.concatenate(pieces, axis=1),
            jnp.concatenate(weights, axis=0),
            preferred_element_type=F32,
        )

    def plane_values(layer, m, phase, g, acc):
        spacing = 2**layer
        rows = spacing * NY
        mask = col_mask(8 * g + phase + ORIGIN[layer + 1], 2, 4)
        bias = rows_ref[8 + layer : 9 + layer, : 4 * C]
        at = (phase * GROUPS[layer + 1] + g) * rows
        values = []
        for b in range(2):
            if COLSTEP[layer] < 4:
                centre = centred(layer, phase, g, b, 1 + m, rows)
            else:
                centre = acts[layer][1, phase, g + 1, b, :, 1 + m].reshape(rows, 4 * C).astype(F32)
            half = acc[at : at + rows, 4 * C * b : 4 * C * (b + 1)] + bias
            values.append(centre + jnp.maximum(half, 0.0) * mask)
        return values

    def plane_finish(layer, m, acc):
        spacing = 2**layer
        for phase in range(2):
            for g in range(GROUPS[layer + 1]):
                for b, value in enumerate(plane_values(layer, m, phase, g, acc)):
                    store_plane(layer + 1, phase, g, spacing * b, spacing, m, value)

    def head_finish(m, acc):
        layer = LAYERS - 1
        spacing = 2**layer
        for phase in range(2):
            last = jnp.concatenate(plane_values(layer, m, phase, 0, acc), axis=1)
            last = last.reshape(spacing, row_parts, NY // row_parts, 8 * C)
            last = last.transpose(1, 0, 2, 3).reshape(spacing * NY, 8 * C).astype(BF)
            heads = lax.dot_general(
                rows_ref[16:24].astype(BF),
                last,
                (((1,), (1,)), ((), ())),
                preferred_element_type=F32,
            )
            size = spacing * NY // row_parts
            for y in range(row_parts):
                for b in range(2):
                    for x in range(4):
                        out_ref[
                            (2 * m + b) * row_parts + y, 2 * x + phase : 2 * x + phase + 1, 0:size
                        ] = heads[4 * b + x : 4 * b + x + 1, y * size : (y + 1) * size]

    def in_line(count, dot, finish):
        for k in range(count):
            finish(k, dot(k))

    fetches[0].wait()
    in_line(GROUPS[0] // 2, stem_dot, stem_finish)
    for layer in range(LAYERS):
        fetches[1 + layer].wait()
        if layer + 1 < LAYERS:
            clear_edges(layer + 1)
        if layer == 0:
            first_layer()
        elif layer == 1:
            second_layer()
        elif layer == 2:
            in_line(
                NZ // 2 ** (layer + 1),
                functools.partial(plane_dot, layer),
                functools.partial(plane_finish, layer),
            )
        else:
            for m in range(NZ // 2 ** (layer + 1)):
                accs[m][...] = plane_dot(layer, m)
                if m:
                    head_finish(m - 1, accs[m - 1])
            head_finish(m, accs[m])


def vmem():
    return pl.BlockSpec(memory_space=pltpu.VMEM)


def body(
    stacks, offsets, ramp_width, stem_weight, stem_bias, layer_weight, layer_bias, head_weight
):
    depth_b, rows_b, tile_len = stacks.shape
    depth_parts, row_parts = lax.axis_size("gz"), lax.axis_size("gy")
    parts = depth_parts * row_parts
    bricks = lax.axis_size("gx")
    assert (depth_b * depth_parts, rows_b * row_parts, parts * SLAB) == (NZ, NY, BX)
    half = depth_b * rows_b // 2
    smem = pl.BlockSpec(memory_space=pltpu.SMEM)
    pieces = pl.pallas_call(
        functools.partial(pack_kernel, parts=parts, bricks=bricks),
        out_shape=jax.ShapeDtypeStruct((parts * bricks, half, 128), BF),
        in_specs=[smem, vmem()],
        out_specs=vmem(),
    )(offsets, stacks)
    pieces = lax.all_to_all(pieces, ("gz", "gy", "gx"), 0, 0, tiled=True)
    pieces = pieces.reshape(depth_parts, row_parts, bricks, half, 128)

    hbm = pl.BlockSpec(memory_space=pltpu.HBM)
    small = jax.ShapeDtypeStruct((24, 8 * C), F32)
    shapes = [jax.ShapeDtypeStruct((GROUPS[0] // 2, 384, 8 * C), BF)] + [
        jax.ShapeDtypeStruct(weight_shape(layer), BF) for layer in range(LAYERS)
    ]
    spaces = [pltpu.VMEM(shape.shape, shape.dtype) for shape in shapes]
    raw = (layer_weight, layer_bias, stem_weight, stem_bias[None], head_weight[None])
    rows, *weights = pl.pallas_call(
        weights_kernel,
        out_shape=[small] + shapes,
        in_specs=[hbm] * 5,
        out_specs=[vmem()] + [hbm] * 5,
        scratch_shapes=[pltpu.VMEM(array.shape, array.dtype) for array in raw]
        + spaces
        + [
            pltpu.VMEM((27, C, 4 * C), F32),
            pltpu.SemaphoreType.DMA((5,)),
            pltpu.SemaphoreType.DMA((5,)),
        ],
        compiler_params=pltpu.CompilerParams(vmem_limit_bytes=64 * 2**20 - 2**18),
        cost_estimate=pl.CostEstimate(flops=4000000, bytes_accessed=9000000, transcendentals=0),
    )(*raw)

    held = [max(act_rows(layer) for layer in range(odd, LAYERS, 2)) for odd in range(2)]
    scratch = (
        spaces
        + [pltpu.VMEM((2, NZ + 2, NY, 128), BF)]
        + [pltpu.VMEM((size, NY, 4 * C), BF) for size in held]
        + [pltpu.VMEM((NZ * NY // 2, 8 * C), F32)] * 2
        + [pltpu.SemaphoreType.DMA((5,))]
        + [pltpu.VMEM(edge_shape(layer), BF) for layer in range(PACKED)]
    )
    logits = pl.pallas_call(
        conv_kernel,
        out_shape=jax.ShapeDtypeStruct((parts, SLAB, 128), F32),
        in_specs=[smem, smem, vmem(), vmem()] + [hbm] * 5,
        out_specs=vmem(),
        scratch_shapes=scratch,
        compiler_params=pltpu.CompilerParams(vmem_limit_bytes=64 * 2**20 - 2**18),
        cost_estimate=pl.CostEstimate(
            flops=20000000000, bytes_accessed=9000000, transcendentals=0
        ),
    )(offsets, ramp_width, pieces, rows, *weights)
    logits = lax.all_to_all(logits, ("gz", "gy"), 0, 0, tiled=True)
    logits = pl.pallas_call(
        unpack_kernel,
        out_shape=jax.ShapeDtypeStruct((depth_b * rows_b, BX), F32),
        in_specs=[vmem()],
        out_specs=vmem(),
    )(logits)
    return logits.reshape(depth_b, rows_b, BX)


def solution(mesh):
    return jax.shard_map(
        body,
        mesh=mesh,
        in_specs=(P("gz", "gy", "gx"), P(), P(), P(), P(), P(), P(), P()),
        out_specs=P("gz", "gy", "gx"),
        check_vma=False,
    )
```

```python
import functools
import math

import jax
import jax.numpy as jnp
from jax import lax
from jax.experimental import pallas as pl
from jax.experimental.pallas import tpu as pltpu
from jax.sharding import PartitionSpec as P

LAYERS = 4
H = 64
S = 32
BX = 128
C = 32
REACH = 16
SLAB = 8
WIDE = SLAB + 2 * REACH
NZ = 32
NY = 32
GROUPS = (10, 5, 4, 3, 1)
PHASES = (1, 2, 2, 2, 2)
TAPS = (2, 2, 2, 3)
COLSTEP = (1, 1, 2, 4)
PACKED = 2
ORIGIN = (-15, -14, -12, -8, 0)
BF = jnp.bfloat16
F32 = jnp.float32


def repeated(row, copies):
    return jnp.concatenate([row] * copies, axis=1)


def weights_kernel(*refs):
    sources, rows_ref, outs, refs = refs[:5], refs[5], refs[6:11], refs[11:]
    inputs, built, turned, in_sems, out_sems = refs[:5], refs[5:10], *refs[10:]
    fetches = [
        pltpu.make_async_copy(a, b, in_sems.at[k]) for k, (a, b) in enumerate(zip(sources, inputs))
    ]
    stores = [
        pltpu.make_async_copy(a, b, out_sems.at[k]) for k, (a, b) in enumerate(zip(built, outs))
    ]
    for copy in fetches:
        copy.start()
    for copy in fetches:
        copy.wait()
    lw_ref, lb_ref, sw_ref, sb_ref, head_ref = inputs
    ws_ref, w_refs = built[0], built[1:]
    lane = lax.broadcasted_iota(jnp.int32, (C, 4 * C), 1) // C
    zero = jnp.zeros((C, 4 * C), BF)
    for layer in range(LAYERS):
        spacing = 2**layer
        out = w_refs[layer]
        flat = lw_ref[layer].astype(F32).reshape(27 * C, C)
        flat = jnp.concatenate([flat, jnp.zeros((28 * 4 * C - 27 * C, C), F32)], axis=0)
        flat = jnp.concatenate([flat, jnp.zeros((28 * 4 * C, 3 * C), F32)], axis=1)
        for t in range(27):
            turned[t] = flat[C * t : C * t + 4 * C].T[:C]

        def per_row_tap(s, carry, layer=layer, spacing=spacing, out=out):
            taps = []
            for c in range(3):
                taps.append([])
                for a in range(3):
                    block = jnp.where(lane == 0, turned[9 * c + a + 3 * s], 0.0)
                    block = block + pltpu.roll(block, 2 * C, 1)
                    taps[c].append(block + pltpu.roll(block, C, 1))
            def place(i, t, xi, b, block):
                lanes = slice(4 * C * b, 4 * C * (b + 1))
                if layer >= PACKED:
                    out[s, i, t, xi * C : (xi + 1) * C, lanes] = block
                elif i == 0:
                    out[s, t, xi * C : (xi + 1) * C, lanes] = block
                else:
                    first = 2 * C * (t % 2) + xi * C
                    out[s, 4 + t // 2, first : first + C, lanes] = block

            for i in range(TAPS[layer]):
                for xi in range(4 if i == 0 or layer >= PACKED else 2):
                    for c in range(3):
                        block = jnp.zeros((C, 4 * C), F32)
                        for a in range(3):
                            xo = 4 * i + xi - COLSTEP[layer] * a
                            if 0 <= xo < 4:
                                block = jnp.where(lane == xo, taps[c][a], block)
                        block = block.astype(BF)
                        for b in range(2):
                            place(i, c + b, xi, b, block)
                    place(i, 0, xi, 1, zero)
                    place(i, 3, xi, 0, zero)
            return carry

        lax.fori_loop(0, 3, per_row_tap, 0)
        stores[1 + layer].start()
    row = lax.broadcasted_iota(jnp.int32, (128, 8 * C), 0)
    column = lax.broadcasted_iota(jnp.int32, (128, 8 * C), 1) // C
    stem = repeated(sw_ref[...].astype(F32), 8)

    def per_tile(k, carry):
        diff = row - column - 8 * k
        for c in range(3):
            block = jnp.zeros((128, 8 * C), F32)
            for b in range(3):
                for a in range(3):
                    tap = 9 * c + 3 * b + a
                    block = jnp.where(diff == WIDE * b + a, stem[tap : tap + 1, :], block)
            ws_ref[k, 128 * c : 128 * (c + 1), :] = block.astype(BF)
        return carry

    lax.fori_loop(0, GROUPS[0] // 2, per_tile, 0)
    stores[0].start()
    rows_ref[...] = jnp.zeros(rows_ref.shape, F32)
    rows_ref[0:1, :] = repeated(sb_ref[...], 8)
    for layer in range(LAYERS):
        rows_ref[8 + layer : 9 + layer, :] = repeated(lb_ref[layer : layer + 1], 8)
    head = repeated(head_ref[...].astype(F32), 8)
    spot = lax.broadcasted_iota(jnp.int32, (8, 8 * C), 0)
    rows_ref[16:24, :] = jnp.where(spot == column[:8], head, 0.0)
    for copy in stores:
        copy.wait()


def pack_kernel(off_ref, stacks_ref, out_ref, *, parts, bricks):
    brick = lax.axis_index("gx")
    tile_len = stacks_ref.shape[2]
    rows = out_ref.shape[1]
    values = stacks_ref[...].astype(F32).reshape(2 * rows, tile_len)
    lane = lax.broadcasted_iota(jnp.int32, (rows, 128), 1)
    for other in range(bricks):
        first = other * BX - REACH - (brick * BX - H + off_ref[brick])
        moved = pltpu.roll(values, lax.rem(64 * tile_len - first, tile_len), 1)
        for j in range(parts):
            low = pltpu.roll(moved[:rows], (tile_len - SLAB * j) % tile_len, 1)[:, :128]
            high = pltpu.roll(moved[rows:], (tile_len + 64 - SLAB * j) % tile_len, 1)[:, :128]
            out_ref[j * bricks + other] = jnp.where(lane < 64, low, high).astype(BF)


def blended_slab(off_ref, ramp_ref, pieces_ref, first_col, total_cols, depth_parts, row_parts):
    bricks = lax.axis_size("gx")
    brick = lax.axis_index("gx")
    lane = lax.broadcasted_iota(jnp.int32, (1, 128), 1) % 64
    col = lane + (first_col - REACH)
    numerator = jnp.zeros((depth_parts, row_parts, 32, 128), F32)
    denominator = jnp.zeros((1, 128), F32)
    for step in range(min(bricks, 3)):
        if bricks > 3:
            tile = jnp.clip(brick - 1 + step, 0, bricks - 1)
            real = (brick - 1 + step >= 0) & (brick - 1 + step < bricks)
        else:
            tile, real = step, True
        tile_len = 2 * BX
        spot = col - (tile * BX - H + off_ref[tile])
        inside = (spot >= 0) & (spot < tile_len) & real
        width = ramp_ref[tile].astype(F32)
        spot = spot.astype(F32)
        weight = jnp.minimum(1.0, jnp.minimum((spot + 1.0) / width, (tile_len - spot) / width))
        weight = jnp.where(inside, weight, 0.0)
        denominator = denominator + weight
        values = pieces_ref[:, :, tile].astype(F32)
        numerator = numerator + values * weight
    good = (col >= 0) & (col < total_cols)
    result = jnp.where(good, numerator / jnp.where(good, denominator, 1.0), 0.0)
    zrows = result.reshape(depth_parts, row_parts, 4, 8, 128)
    low = zrows.transpose(0, 2, 1, 3, 4)
    high = pltpu.roll(result.reshape(-1, 128), 64, 1).reshape(zrows.shape).transpose(0, 2, 1, 3, 4)
    image = jnp.stack([low, high], axis=1).reshape(NZ * NY, 128)
    lanes = lax.broadcasted_iota(jnp.int32, image.shape, 1)
    return jnp.where(lanes < WIDE, image, 0.0)


def shifted(value, by):
    planes = value.reshape(-1, NY, value.shape[1])
    blank = jnp.zeros((planes.shape[0], abs(by), value.shape[1]), value.dtype)
    if by > 0:
        moved = jnp.concatenate([blank, planes[:, : NY - by]], axis=1)
    else:
        moved = jnp.concatenate([planes[:, -by:], blank], axis=1)
    return moved.reshape(value.shape)


def weight_shape(layer):
    return (3, 6, 4 * C, 8 * C) if layer < PACKED else (3, TAPS[layer], 4, 4 * C, 8 * C)


def act_shape(layer):
    planes = NZ // 2 ** (layer + 1) + 2
    return (3, PHASES[layer], GROUPS[layer], 2, 2**layer, planes, NY, 4 * C)


def edge_shape(layer):
    planes = NZ // 2 ** (layer + 1) + 1
    return (3, PHASES[layer], GROUPS[layer] - 1, 2**layer, planes, NY, 4 * C)


def act_rows(layer):
    return math.prod(act_shape(layer)[:-2])


def conv_kernel(off_ref, ramp_ref, pieces_ref, rows_ref, *refs):
    built, out_ref, refs = refs[:5], refs[5], refs[6:]
    held, stem_in, spaces, accs = refs[:5], refs[5], refs[6:8], refs[8:10]
    sems, edges = refs[10], refs[11:]
    fetches = [
        pltpu.make_async_copy(a, b, sems.at[k]) for k, (a, b) in enumerate(zip(built, held))
    ]
    for copy in fetches:
        copy.start()
    ws_ref, w_refs = held[0], held[1:]
    acts = [
        spaces[layer % 2].at[0 : act_rows(layer)].reshape(act_shape(layer))
        for layer in range(LAYERS)
    ]
    depth_parts, row_parts = lax.axis_size("gz"), lax.axis_size("gy")
    slab = lax.axis_index("gz") * row_parts + lax.axis_index("gy")
    first_col = lax.axis_index("gx") * BX + slab * SLAB
    total_cols = lax.axis_size("gx") * BX

    def col_mask(start, step, width):
        lane = lax.broadcasted_iota(jnp.int32, (1, width * C), 1) // C
        col = step * lane + (first_col + start)
        return jnp.where((col >= 0) & (col < total_cols), 1.0, 0.0)

    def clear_edges(layer):
        spacing = 2**layer
        pad = jnp.zeros((3, spacing, NY, 4 * C), BF)
        for phase in range(PHASES[layer]):
            for g in range(GROUPS[layer]):
                acts[layer][:, phase, g, 1, :, 0] = pad
                acts[layer][:, phase, g, 0, :, NZ // (2 * spacing) + 1] = pad

    def store(layer, phase, group, start, length, value):
        spacing = 2**layer
        rows = slice(start, start + length)
        for s in range(3):
            part = value if s == 1 else shifted(value, spacing if s == 0 else -spacing)
            planes = part.astype(BF).reshape(length, -1, 2, NY, 4 * C)
            count = planes.shape[1]
            low, high = planes[:, :, 0], planes[:, :, 1]
            acts[layer][s, phase, group, 0, rows, 1 : 1 + count] = low
            acts[layer][s, phase, group, 1, rows, 1 : 1 + count] = high
            if layer < PACKED and group > 0:
                low, high = low[..., : 2 * C], high[..., : 2 * C]
                blank = jnp.zeros((length, 1, NY, 2 * C), BF)
                out = edges[layer]
                first = jnp.concatenate([blank, low[:, :1]], axis=-1)
                inner = jnp.concatenate([high[:, :-1], low[:, 1:]], axis=-1)
                last = jnp.concatenate([high[:, -1:], blank], axis=-1)
                out[s, phase, group - 1, rows, 0:1] = first
                out[s, phase, group - 1, rows, 1:count] = inner
                out[s, phase, group - 1, rows, count : count + 1] = last

    def store_plane(layer, phase, group, start, length, m, value):
        spacing = 2**layer
        for s in range(3):
            part = value if s == 1 else shifted(value, spacing if s == 0 else -spacing)
            planes = part.astype(BF).reshape(length, NY, 4 * C)
            acts[layer][s, phase, group, m % 2, start : start + length, 1 + m // 2] = planes

    clear_edges(0)
    clear_edges(1)
    image = blended_slab(
        off_ref, ramp_ref, pieces_ref, first_col, total_cols, depth_parts, row_parts
    )
    packed = shifted(image, 1)
    packed = packed + pltpu.roll(image, WIDE, 1)
    packed = packed + pltpu.roll(shifted(image, -1), 2 * WIDE, 1)
    coarse = packed.astype(BF)
    fine = (packed - coarse.astype(F32)).astype(BF)
    for part, value in enumerate((coarse, fine)):
        stem_in[part, 0] = jnp.zeros((NY, 128), BF)
        stem_in[part, NZ + 1] = jnp.zeros((NY, 128), BF)
        stem_in[part, 1 : NZ + 1] = value.reshape(NZ, NY, 128)

    def stem_dot(k):
        lhs = jnp.concatenate(
            [stem_in[p, c : c + NZ].reshape(NZ * NY, 128) for p in range(2) for c in range(3)],
            axis=1,
        )
        weights = jnp.concatenate([ws_ref[k], ws_ref[k]], axis=0)
        return jnp.dot(lhs, weights, preferred_element_type=F32)

    def stem_finish(k, acc):
        mask = col_mask(8 * k + ORIGIN[0], 1, 8)
        value = jnp.maximum(acc + rows_ref[0:1], 0.0) * mask
        store(0, 0, 2 * k, 0, 1, value[:, : 4 * C])
        store(0, 0, 2 * k + 1, 0, 1, value[:, 4 * C :])

    def group_dot(layer, phase, g):
        spacing = 2**layer
        count = NZ // (2 * spacing)
        rows = NZ * NY // 2
        pieces = []
        for s in range(3):
            for t in range(4):
                start = (t + 1) // 2
                piece = acts[layer][s, phase, g, 1 - t % 2, :, start : start + count]
                pieces.append(piece.reshape(rows, 4 * C))
            for start in range(2):
                piece = edges[layer][s, phase, g, :, start : start + count]
                pieces.append(piece.reshape(rows, 4 * C))
        lhs = jnp.concatenate(pieces, axis=1)
        weights = w_refs[layer][...].reshape(18 * 4 * C, 8 * C)
        return jnp.dot(lhs, weights, preferred_element_type=F32)

    def centred(layer, phase, g, b, planes, rows):
        near = [acts[layer][1, phase, g + i, b, :, planes].reshape(rows, 4 * C) for i in range(2)]
        pair = jnp.concatenate(near, axis=1)
        first = COLSTEP[layer] * C
        return pair[:, first : first + 4 * C].astype(F32)

    def group_values(layer, phase, g, acc, mask):
        count = NZ // (2 * 2**layer)
        bias = rows_ref[8 + layer : 9 + layer, : 4 * C]
        values = []
        for b in range(2):
            centre = centred(layer, phase, g, b, slice(1, 1 + count), NZ * NY // 2)
            half = acc[:, 4 * C * b : 4 * C * (b + 1)] + bias
            values.append(centre + jnp.maximum(half, 0.0) * mask)
        return values

    def split_store(k, left, right):
        for b in range(2):
            one = left[b]
            block = lax.broadcasted_iota(jnp.int32, one.shape, 1) // C
            up, far = pltpu.roll(one, 3 * C, 1), pltpu.roll(one, 2 * C, 1)
            even = jnp.where(block == 0, one, up)
            odd = jnp.where(block == 0, up, far)
            if right is None:
                even_end = odd_end = jnp.zeros_like(one)
            else:
                two = right[b]
                down, far = pltpu.roll(two, C, 1), pltpu.roll(two, 2 * C, 1)
                even_end = jnp.where(block == 2, far, down)
                odd_end = jnp.where(block == 2, down, two)
            store(1, 0, k, b, 1, jnp.where(block < 2, even, even_end))
            store(1, 1, k, b, 1, jnp.where(block < 2, odd, odd_end))

    def first_layer():
        left = None
        for g in range(GROUPS[0] - 1):
            mask = col_mask(4 * g + ORIGIN[1], 1, 4)
            values = group_values(0, 0, g, group_dot(0, 0, g), mask)
            if left is None:
                left = values
            else:
                split_store(g // 2, left, values)
                left = None
        split_store(GROUPS[1] - 1, left, None)

    def second_layer():
        order = [(phase, g) for phase in range(2) for g in range(GROUPS[2])]
        order.sort(key=lambda pair: pair[1] == GROUPS[2] - 1)
        for phase, g in order:
            mask = col_mask(8 * g + phase + ORIGIN[2], 2, 4)
            values = group_values(1, phase, g, group_dot(1, phase, g), mask)
            for b in range(2):
                store(2, phase, g, 2 * b, 2, values[b])

    def plane_dot(layer, m):
        spacing = 2**layer
        groups = GROUPS[layer + 1]
        taps = [t for t in range(4) if 0 < m + (t + 1) // 2 < NZ // (2 * spacing) + 1]
        pieces, weights = [], []
        for s in range(3):
            for i in range(TAPS[layer]):
                for t in taps:
                    piece = acts[layer][s, :, i : i + groups, 1 - t % 2, :, m + (t + 1) // 2]
                    pieces.append(piece.reshape(2 * groups * spacing * NY, 4 * C))
                    weights.append(w_refs[layer][s, i, t])
        return jnp.dot(
            jnp.concatenate(pieces, axis=1),
            jnp.concatenate(weights, axis=0),
            preferred_element_type=F32,
        )

    def plane_values(layer, m, phase, g, acc):
        spacing = 2**layer
        rows = spacing * NY
        mask = col_mask(8 * g + phase + ORIGIN[layer + 1], 2, 4)
        bias = rows_ref[8 + layer : 9 + layer, : 4 * C]
        at = (phase * GROUPS[layer + 1] + g) * rows
        values = []
        for b in range(2):
            if COLSTEP[layer] < 4:
                centre = centred(layer, phase, g, b, 1 + m, rows)
            else:
                centre = acts[layer][1, phase, g + 1, b, :, 1 + m].reshape(rows, 4 * C).astype(F32)
            half = acc[at : at + rows, 4 * C * b : 4 * C * (b + 1)] + bias
            values.append(centre + jnp.maximum(half, 0.0) * mask)
        return values

    def plane_finish(layer, m, acc):
        spacing = 2**layer
        for phase in range(2):
            for g in range(GROUPS[layer + 1]):
                for b, value in enumerate(plane_values(layer, m, phase, g, acc)):
                    store_plane(layer + 1, phase, g, spacing * b, spacing, m, value)

    def head_finish(m, acc):
        layer = LAYERS - 1
        spacing = 2**layer
        for phase in range(2):
            last = jnp.concatenate(plane_values(layer, m, phase, 0, acc), axis=1)
            last = last.reshape(spacing, row_parts, NY // row_parts, 8 * C)
            last = last.transpose(1, 0, 2, 3).reshape(spacing * NY, 8 * C).astype(BF)
            heads = lax.dot_general(
                rows_ref[16:24].astype(BF),
                last,
                (((1,), (1,)), ((), ())),
                preferred_element_type=F32,
            )
            size = spacing * NY // row_parts
            for y in range(row_parts):
                for b in range(2):
                    for x in range(4):
                        out_ref[
                            (2 * m + b) * row_parts + y, 2 * x + phase : 2 * x + phase + 1, 0:size
                        ] = heads[4 * b + x : 4 * b + x + 1, y * size : (y + 1) * size]

    def in_line(count, dot, finish):
        for k in range(count):
            finish(k, dot(k))

    fetches[0].wait()
    for k in range(GROUPS[0] // 2):
        if k == GROUPS[0] // 2 - 1:
            for copy in fetches[1:]:
                copy.wait()
        stem_finish(k, stem_dot(k))
    for layer in range(LAYERS):
        if layer == 0:
            first_layer()
        elif layer == 1:
            second_layer()
        elif layer == 2:
            in_line(
                NZ // 2 ** (layer + 1),
                functools.partial(plane_dot, layer),
                functools.partial(plane_finish, layer),
            )
        else:
            for m in range(NZ // 2 ** (layer + 1)):
                accs[m][...] = plane_dot(layer, m)
                if m:
                    head_finish(m - 1, accs[m - 1])
            head_finish(m, accs[m])


def vmem():
    return pl.BlockSpec(memory_space=pltpu.VMEM)


def body(
    stacks, offsets, ramp_width, stem_weight, stem_bias, layer_weight, layer_bias, head_weight
):
    depth_b, rows_b, tile_len = stacks.shape
    depth_parts, row_parts = lax.axis_size("gz"), lax.axis_size("gy")
    parts = depth_parts * row_parts
    bricks = lax.axis_size("gx")
    assert (depth_b * depth_parts, rows_b * row_parts, parts * SLAB) == (NZ, NY, BX)
    half = depth_b * rows_b // 2
    smem = pl.BlockSpec(memory_space=pltpu.SMEM)
    pieces = pl.pallas_call(
        functools.partial(pack_kernel, parts=parts, bricks=bricks),
        out_shape=jax.ShapeDtypeStruct((parts * bricks, half, 128), BF),
        in_specs=[smem, vmem()],
        out_specs=vmem(),
    )(offsets, stacks)
    pieces = lax.all_to_all(pieces, ("gz", "gy", "gx"), 0, 0, tiled=True)
    pieces = pieces.reshape(depth_parts, row_parts, bricks, half, 128)

    hbm = pl.BlockSpec(memory_space=pltpu.HBM)
    small = jax.ShapeDtypeStruct((24, 8 * C), F32)
    shapes = [jax.ShapeDtypeStruct((GROUPS[0] // 2, 384, 8 * C), BF)] + [
        jax.ShapeDtypeStruct(weight_shape(layer), BF) for layer in range(LAYERS)
    ]
    spaces = [pltpu.VMEM(shape.shape, shape.dtype) for shape in shapes]
    raw = (layer_weight, layer_bias, stem_weight, stem_bias[None], head_weight[None])
    rows, *weights = pl.pallas_call(
        weights_kernel,
        out_shape=[small] + shapes,
        in_specs=[hbm] * 5,
        out_specs=[vmem()] + [hbm] * 5,
        scratch_shapes=[pltpu.VMEM(array.shape, array.dtype) for array in raw]
        + spaces
        + [
            pltpu.VMEM((27, C, 4 * C), F32),
            pltpu.SemaphoreType.DMA((5,)),
            pltpu.SemaphoreType.DMA((5,)),
        ],
        compiler_params=pltpu.CompilerParams(vmem_limit_bytes=64 * 2**20 - 2**18),
        cost_estimate=pl.CostEstimate(flops=4000000, bytes_accessed=9000000, transcendentals=0),
    )(*raw)

    held = [max(act_rows(layer) for layer in range(odd, LAYERS, 2)) for odd in range(2)]
    scratch = (
        spaces
        + [pltpu.VMEM((2, NZ + 2, NY, 128), BF)]
        + [pltpu.VMEM((size, NY, 4 * C), BF) for size in held]
        + [pltpu.VMEM((NZ * NY // 2, 8 * C), F32)] * 2
        + [pltpu.SemaphoreType.DMA((5,))]
        + [pltpu.VMEM(edge_shape(layer), BF) for layer in range(PACKED)]
    )
    logits = pl.pallas_call(
        conv_kernel,
        out_shape=jax.ShapeDtypeStruct((parts, SLAB, 128), F32),
        in_specs=[smem, smem, vmem(), vmem()] + [hbm] * 5,
        out_specs=vmem(),
        scratch_shapes=scratch,
        compiler_params=pltpu.CompilerParams(vmem_limit_bytes=64 * 2**20 - 2**18),
        cost_estimate=pl.CostEstimate(
            flops=20000000000, bytes_accessed=9000000, transcendentals=0
        ),
    )(offsets, ramp_width, pieces, rows, *weights)
    logits = lax.all_to_all(logits, ("gz", "gy"), 0, 0, tiled=True)
    logits = logits[:, :, : depth_b * rows_b].transpose(2, 0, 1)
    return logits.reshape(depth_b, rows_b, BX)


def solution(mesh):
    return jax.shard_map(
        body,
        mesh=mesh,
        in_specs=(P("gz", "gy", "gx"), P(), P(), P(), P(), P(), P(), P()),
        out_specs=P("gz", "gy", "gx"),
        check_vma=False,
    )
```

```python
import functools
import math

import jax
import jax.numpy as jnp
from jax import lax
from jax.experimental import pallas as pl
from jax.experimental.pallas import tpu as pltpu
from jax.sharding import PartitionSpec as P

LAYERS = 4
H = 64
S = 32
BX = 128
C = 32
REACH = 16
SLAB = 8
WIDE = SLAB + 2 * REACH
NZ = 32
DEPTHS = (0, 3, 5)
NY = 32
GROUPS = (10, 5, 4, 3, 1)
PHASES = (1, 2, 2, 2, 2)
TAPS = (2, 2, 2, 3)
COLSTEP = (1, 1, 2, 4)
PACKED = 2
ORIGIN = (-15, -14, -12, -8, 0)
BF = jnp.bfloat16
F32 = jnp.float32


def repeated(row, copies):
    return jnp.concatenate([row] * copies, axis=1)


def weights_kernel(*refs):
    sources, rows_ref, outs, refs = refs[:5], refs[5], refs[6:11], refs[11:]
    inputs, built, turned, in_sems, out_sems = refs[:5], refs[5:10], *refs[10:]
    fetches = [
        pltpu.make_async_copy(a, b, in_sems.at[k]) for k, (a, b) in enumerate(zip(sources, inputs))
    ]
    stores = [
        pltpu.make_async_copy(a, b, out_sems.at[k]) for k, (a, b) in enumerate(zip(built, outs))
    ]
    for copy in fetches:
        copy.start()
    for copy in fetches:
        copy.wait()
    lw_ref, lb_ref, sw_ref, sb_ref, head_ref = inputs
    ws_ref, w_refs = built[0], built[1:]
    lane = lax.broadcasted_iota(jnp.int32, (C, 4 * C), 1) // C
    zero = jnp.zeros((C, 4 * C), BF)
    for layer in range(LAYERS):
        spacing = 2**layer
        out = w_refs[layer]
        flat = lw_ref[layer].astype(F32).reshape(27 * C, C)
        flat = jnp.concatenate([flat, jnp.zeros((28 * 4 * C - 27 * C, C), F32)], axis=0)
        flat = jnp.concatenate([flat, jnp.zeros((28 * 4 * C, 3 * C), F32)], axis=1)
        for t in range(27):
            turned[t] = flat[C * t : C * t + 4 * C].T[:C]

        def per_row_tap(s, carry, layer=layer, spacing=spacing, out=out):
            taps = []
            for c in range(3):
                taps.append([])
                for a in range(3):
                    block = jnp.where(lane == 0, turned[9 * c + a + 3 * s], 0.0)
                    block = block + pltpu.roll(block, 2 * C, 1)
                    taps[c].append(block + pltpu.roll(block, C, 1))
            def place(i, t, xi, b, block):
                lanes = slice(4 * C * b, 4 * C * (b + 1))
                if layer >= PACKED:
                    out[s, i, t, xi * C : (xi + 1) * C, lanes] = block
                elif i == 0:
                    out[s, t, xi * C : (xi + 1) * C, lanes] = block
                else:
                    first = 2 * C * (t % 2) + xi * C
                    out[s, 4 + t // 2, first : first + C, lanes] = block

            for i in range(TAPS[layer]):
                for xi in range(4 if i == 0 or layer >= PACKED else 2):
                    for c in range(3):
                        block = jnp.zeros((C, 4 * C), F32)
                        for a in range(3):
                            xo = 4 * i + xi - COLSTEP[layer] * a
                            if 0 <= xo < 4:
                                block = jnp.where(lane == xo, taps[c][a], block)
                        block = block.astype(BF)
                        for b in range(2):
                            place(i, c + b, xi, b, block)
                    place(i, 0, xi, 1, zero)
                    place(i, 3, xi, 0, zero)
            return carry

        lax.fori_loop(0, 3, per_row_tap, 0)
        stores[1 + layer].start()
    row = lax.broadcasted_iota(jnp.int32, (128, 8 * C), 0)
    column = lax.broadcasted_iota(jnp.int32, (128, 8 * C), 1) // C
    stem = repeated(sw_ref[...].astype(F32), 8)

    def per_tile(k, carry):
        diff = row - column - 8 * k
        for c in range(3):
            block = jnp.zeros((128, 8 * C), F32)
            for b in range(3):
                for a in range(3):
                    tap = 9 * c + 3 * b + a
                    block = jnp.where(diff == WIDE * b + a, stem[tap : tap + 1, :], block)
            ws_ref[k, 128 * c : 128 * (c + 1), :] = block.astype(BF)
        return carry

    lax.fori_loop(0, GROUPS[0] // 2, per_tile, 0)
    stores[0].start()
    rows_ref[...] = jnp.zeros(rows_ref.shape, F32)
    rows_ref[0:1, :] = repeated(sb_ref[...], 8)
    for layer in range(LAYERS):
        rows_ref[8 + layer : 9 + layer, :] = repeated(lb_ref[layer : layer + 1], 8)
    head = repeated(head_ref[...].astype(F32), 8)
    spot = lax.broadcasted_iota(jnp.int32, (8, 8 * C), 0)
    rows_ref[16:24, :] = jnp.where(spot == column[:8], head, 0.0)
    for copy in stores:
        copy.wait()


def pack_kernel(off_ref, stacks_ref, out_ref, *, parts, bricks):
    brick = lax.axis_index("gx")
    depth, height, tile_len = stacks_ref.shape
    rows = 3 * height
    values = stacks_ref[...].astype(F32).reshape(depth * height, tile_len)
    lane = lax.broadcasted_iota(jnp.int32, (rows, 128), 1)
    turned = []
    for other in range(bricks):
        first = other * BX - REACH - (brick * BX - H + off_ref[brick])
        turned.append(pltpu.roll(values, lax.rem(64 * tile_len - first, tile_len), 1))
    for j in range(parts):
        messages = []
        for moved in turned:
            blocks = []
            for k, z in enumerate(DEPTHS):
                block = moved[z * height : z * height + rows]
                by = (tile_len + WIDE * k - SLAB * j) % tile_len
                blocks.append(pltpu.roll(block, by, 1)[:, :128])
            later = jnp.where(lane < 2 * WIDE, blocks[1], blocks[2])
            messages.append(jnp.where(lane < WIDE, blocks[0], later))
        message = jnp.concatenate(messages, axis=0).astype(BF)
        out_ref[j * bricks * rows : (j + 1) * bricks * rows] = message


def blended_slab(off_ref, ramp_ref, pieces_ref, first_col, total_cols, depth_parts, row_parts):
    bricks = lax.axis_size("gx")
    lane = lax.broadcasted_iota(jnp.int32, (1, 128), 1)
    lane = jnp.where(lane < WIDE, lane, jnp.where(lane < 2 * WIDE, lane - WIDE, lane - 2 * WIDE))
    col = lane + (first_col - REACH)
    height = NY // row_parts
    pieces = pieces_ref[...].astype(F32)
    pieces = pieces.reshape(depth_parts, row_parts, bricks, 3 * height, 128)
    numerator = jnp.zeros((depth_parts, row_parts, 3 * height, 128), F32)
    denominator = jnp.zeros((1, 128), F32)
    for tile in range(bricks):
        tile_len = 2 * BX
        spot = col - (tile * BX - H + off_ref[tile])
        inside = (spot >= 0) & (spot < tile_len)
        width = ramp_ref[tile].astype(F32)
        spot = spot.astype(F32)
        weight = jnp.minimum(1.0, jnp.minimum((spot + 1.0) / width, (tile_len - spot) / width))
        weight = jnp.where(inside, weight, 0.0)
        denominator = denominator + weight
        numerator = numerator + pieces[:, :, tile] * weight
    good = (col >= 0) & (col < total_cols)
    result = jnp.where(good, numerator / jnp.where(good, denominator, 1.0), 0.0)
    blocks = []
    for k in range(3):
        block = result.reshape(-1, 128)
        if k:
            block = pltpu.roll(block, 128 - WIDE * k, 1)
        block = block.reshape(depth_parts, row_parts, 3, height, 128)
        blocks.append(block if k < 2 else block[:, :, 1:])
    image = jnp.concatenate(blocks, axis=2).transpose(0, 2, 1, 3, 4).reshape(NZ * NY, 128)
    lanes = lax.broadcasted_iota(jnp.int32, image.shape, 1)
    return jnp.where(lanes < WIDE, image, 0.0)


def shifted(value, by):
    planes = value.reshape(-1, NY, value.shape[1])
    blank = jnp.zeros((planes.shape[0], abs(by), value.shape[1]), value.dtype)
    if by > 0:
        moved = jnp.concatenate([blank, planes[:, : NY - by]], axis=1)
    else:
        moved = jnp.concatenate([planes[:, -by:], blank], axis=1)
    return moved.reshape(value.shape)


def weight_shape(layer):
    return (3, 6, 4 * C, 8 * C) if layer < PACKED else (3, TAPS[layer], 4, 4 * C, 8 * C)


def act_shape(layer):
    planes = NZ // 2 ** (layer + 1) + 2
    return (3, PHASES[layer], GROUPS[layer], 2, 2**layer, planes, NY, 4 * C)


def edge_shape(layer):
    planes = NZ // 2 ** (layer + 1) + 1
    return (3, PHASES[layer], GROUPS[layer] - 1, 2**layer, planes, NY, 4 * C)


def act_rows(layer):
    return math.prod(act_shape(layer)[:-2])


def conv_kernel(off_ref, ramp_ref, pieces_ref, rows_ref, *refs):
    built, out_ref, refs = refs[:5], refs[5], refs[6:]
    held, stem_in, spaces, accs = refs[:5], refs[5], refs[6:8], refs[8:10]
    sems, edges = refs[10], refs[11:]
    fetches = [
        pltpu.make_async_copy(a, b, sems.at[k]) for k, (a, b) in enumerate(zip(built, held))
    ]
    for copy in fetches:
        copy.start()
    ws_ref, w_refs = held[0], held[1:]
    acts = [
        spaces[layer % 2].at[0 : act_rows(layer)].reshape(act_shape(layer))
        for layer in range(LAYERS)
    ]
    depth_parts, row_parts = lax.axis_size("gz"), lax.axis_size("gy")
    slab = lax.axis_index("gz") * row_parts + lax.axis_index("gy")
    first_col = lax.axis_index("gx") * BX + slab * SLAB
    total_cols = lax.axis_size("gx") * BX

    def col_mask(start, step, width):
        lane = lax.broadcasted_iota(jnp.int32, (1, width * C), 1) // C
        col = step * lane + (first_col + start)
        return jnp.where((col >= 0) & (col < total_cols), 1.0, 0.0)

    def clear_edges(layer):
        spacing = 2**layer
        pad = jnp.zeros((3, spacing, NY, 4 * C), BF)
        for phase in range(PHASES[layer]):
            for g in range(GROUPS[layer]):
                acts[layer][:, phase, g, 1, :, 0] = pad
                acts[layer][:, phase, g, 0, :, NZ // (2 * spacing) + 1] = pad

    def store(layer, phase, group, start, length, value):
        spacing = 2**layer
        rows = slice(start, start + length)
        for s in range(3):
            part = value if s == 1 else shifted(value, spacing if s == 0 else -spacing)
            planes = part.astype(BF).reshape(length, -1, 2, NY, 4 * C)
            count = planes.shape[1]
            low, high = planes[:, :, 0], planes[:, :, 1]
            acts[layer][s, phase, group, 0, rows, 1 : 1 + count] = low
            acts[layer][s, phase, group, 1, rows, 1 : 1 + count] = high
            if layer < PACKED and group > 0:
                low, high = low[..., : 2 * C], high[..., : 2 * C]
                blank = jnp.zeros((length, 1, NY, 2 * C), BF)
                out = edges[layer]
                first = jnp.concatenate([blank, low[:, :1]], axis=-1)
                inner = jnp.concatenate([high[:, :-1], low[:, 1:]], axis=-1)
                last = jnp.concatenate([high[:, -1:], blank], axis=-1)
                out[s, phase, group - 1, rows, 0:1] = first
                out[s, phase, group - 1, rows, 1:count] = inner
                out[s, phase, group - 1, rows, count : count + 1] = last

    def store_plane(layer, phase, group, start, length, m, value):
        spacing = 2**layer
        for s in range(3):
            part = value if s == 1 else shifted(value, spacing if s == 0 else -spacing)
            planes = part.astype(BF).reshape(length, NY, 4 * C)
            acts[layer][s, phase, group, m % 2, start : start + length, 1 + m // 2] = planes

    clear_edges(0)
    clear_edges(1)
    image = blended_slab(
        off_ref, ramp_ref, pieces_ref, first_col, total_cols, depth_parts, row_parts
    )
    packed = shifted(image, 1)
    packed = packed + pltpu.roll(image, WIDE, 1)
    packed = packed + pltpu.roll(shifted(image, -1), 2 * WIDE, 1)
    coarse = packed.astype(BF)
    fine = (packed - coarse.astype(F32)).astype(BF)
    for part, value in enumerate((coarse, fine)):
        stem_in[part, 0] = jnp.zeros((NY, 128), BF)
        stem_in[part, NZ + 1] = jnp.zeros((NY, 128), BF)
        stem_in[part, 1 : NZ + 1] = value.reshape(NZ, NY, 128)

    def stem_dot(k):
        lhs = jnp.concatenate(
            [stem_in[p, c : c + NZ].reshape(NZ * NY, 128) for p in range(2) for c in range(3)],
            axis=1,
        )
        weights = jnp.concatenate([ws_ref[k], ws_ref[k]], axis=0)
        return jnp.dot(lhs, weights, preferred_element_type=F32)

    def stem_finish(k, acc):
        mask = col_mask(8 * k + ORIGIN[0], 1, 8)
        value = jnp.maximum(acc + rows_ref[0:1], 0.0) * mask
        store(0, 0, 2 * k, 0, 1, value[:, : 4 * C])
        store(0, 0, 2 * k + 1, 0, 1, value[:, 4 * C :])

    def group_dot(layer, phase, g):
        spacing = 2**layer
        count = NZ // (2 * spacing)
        rows = NZ * NY // 2
        pieces = []
        for s in range(3):
            for t in range(4):
                start = (t + 1) // 2
                piece = acts[layer][s, phase, g, 1 - t % 2, :, start : start + count]
                pieces.append(piece.reshape(rows, 4 * C))
            for start in range(2):
                piece = edges[layer][s, phase, g, :, start : start + count]
                pieces.append(piece.reshape(rows, 4 * C))
        lhs = jnp.concatenate(pieces, axis=1)
        weights = w_refs[layer][...].reshape(18 * 4 * C, 8 * C)
        return jnp.dot(lhs, weights, preferred_element_type=F32)

    def centred(layer, phase, g, b, planes, rows):
        near = [acts[layer][1, phase, g + i, b, :, planes].reshape(rows, 4 * C) for i in range(2)]
        pair = jnp.concatenate(near, axis=1)
        first = COLSTEP[layer] * C
        return pair[:, first : first + 4 * C].astype(F32)

    def group_values(layer, phase, g, acc, mask):
        count = NZ // (2 * 2**layer)
        bias = rows_ref[8 + layer : 9 + layer, : 4 * C]
        values = []
        for b in range(2):
            centre = centred(layer, phase, g, b, slice(1, 1 + count), NZ * NY // 2)
            half = acc[:, 4 * C * b : 4 * C * (b + 1)] + bias
            values.append(centre + jnp.maximum(half, 0.0) * mask)
        return values

    def split_store(k, left, right):
        for b in range(2):
            one = left[b]
            block = lax.broadcasted_iota(jnp.int32, one.shape, 1) // C
            up, far = pltpu.roll(one, 3 * C, 1), pltpu.roll(one, 2 * C, 1)
            even = jnp.where(block == 0, one, up)
            odd = jnp.where(block == 0, up, far)
            if right is None:
                even_end = odd_end = jnp.zeros_like(one)
            else:
                two = right[b]
                down, far = pltpu.roll(two, C, 1), pltpu.roll(two, 2 * C, 1)
                even_end = jnp.where(block == 2, far, down)
                odd_end = jnp.where(block == 2, down, two)
            store(1, 0, k, b, 1, jnp.where(block < 2, even, even_end))
            store(1, 1, k, b, 1, jnp.where(block < 2, odd, odd_end))

    def first_layer():
        left = None
        for g in range(GROUPS[0] - 1):
            mask = col_mask(4 * g + ORIGIN[1], 1, 4)
            values = group_values(0, 0, g, group_dot(0, 0, g), mask)
            if left is None:
                left = values
            else:
                split_store(g // 2, left, values)
                left = None
        split_store(GROUPS[1] - 1, left, None)

    def second_layer():
        order = [(phase, g) for phase in range(2) for g in range(GROUPS[2])]
        order.sort(key=lambda pair: pair[1] == GROUPS[2] - 1)
        for phase, g in order:
            mask = col_mask(8 * g + phase + ORIGIN[2], 2, 4)
            values = group_values(1, phase, g, group_dot(1, phase, g), mask)
            for b in range(2):
                store(2, phase, g, 2 * b, 2, values[b])

    def plane_dot(layer, m, first=0, groups=1):
        spacing = 2**layer
        taps = [t for t in range(4) if 0 < m + (t + 1) // 2 < NZ // (2 * spacing) + 1]
        pieces, weights = [], []
        for s in range(3):
            for i in range(TAPS[layer]):
                for t in taps:
                    piece = acts[layer][s, :, i + first : i + first + groups, 1 - t % 2, :, m + (t + 1) // 2]
                    pieces.append(piece.reshape(2 * groups * spacing * NY, 4 * C))
                    weights.append(w_refs[layer][s, i, t])
        return jnp.dot(
            jnp.concatenate(pieces, axis=1),
            jnp.concatenate(weights, axis=0),
            preferred_element_type=F32,
        )

    def plane_values(layer, m, phase, g, acc, first=0, groups=1):
        spacing = 2**layer
        rows = spacing * NY
        mask = col_mask(8 * g + phase + ORIGIN[layer + 1], 2, 4)
        bias = rows_ref[8 + layer : 9 + layer, : 4 * C]
        at = (phase * groups + g - first) * rows
        values = []
        for b in range(2):
            if COLSTEP[layer] < 4:
                centre = centred(layer, phase, g, b, 1 + m, rows)
            else:
                centre = acts[layer][1, phase, g + 1, b, :, 1 + m].reshape(rows, 4 * C).astype(F32)
            half = acc[at : at + rows, 4 * C * b : 4 * C * (b + 1)] + bias
            values.append(centre + jnp.maximum(half, 0.0) * mask)
        return values

    def plane_finish(layer, m, first, groups, acc):
        spacing = 2**layer
        for phase in range(2):
            for g in range(first, first + groups):
                values = plane_values(layer, m, phase, g, acc, first, groups)
                for b, value in enumerate(values):
                    store_plane(layer + 1, phase, g, spacing * b, spacing, m, value)

    def head_finish(m, acc):
        layer = LAYERS - 1
        spacing = 2**layer
        for phase in range(2):
            last = jnp.concatenate(plane_values(layer, m, phase, 0, acc), axis=1)
            last = last.reshape(spacing, row_parts, NY // row_parts, 8 * C)
            last = last.transpose(1, 0, 2, 3).reshape(spacing * NY, 8 * C).astype(BF)
            heads = lax.dot_general(
                rows_ref[16:24].astype(BF),
                last,
                (((1,), (1,)), ((), ())),
                preferred_element_type=F32,
            )
            size = spacing * NY // row_parts
            for y in range(row_parts):
                for b in range(2):
                    for x in range(4):
                        out_ref[
                            (2 * m + b) * row_parts + y, 2 * x + phase : 2 * x + phase + 1, 0:size
                        ] = heads[4 * b + x : 4 * b + x + 1, y * size : (y + 1) * size]

    fetches[0].wait()
    for k in range(GROUPS[0] // 2):
        if k == GROUPS[0] // 2 - 1:
            for copy in fetches[1:]:
                copy.wait()
        stem_finish(k, stem_dot(k))
    for layer in range(LAYERS):
        if layer == 0:
            first_layer()
        elif layer == 1:
            second_layer()
        elif layer == 2:
            for first, groups in ((0, GROUPS[3] - 1), (GROUPS[3] - 1, 1)):
                for m in range(NZ // 2 ** (layer + 1)):
                    plane_finish(layer, m, first, groups, plane_dot(layer, m, first, groups))
        else:
            for m in range(NZ // 2 ** (layer + 1)):
                accs[m][...] = plane_dot(layer, m)
                if m:
                    head_finish(m - 1, accs[m - 1])
            head_finish(m, accs[m])


def vmem():
    return pl.BlockSpec(memory_space=pltpu.VMEM)


def body(
    stacks, offsets, ramp_width, stem_weight, stem_bias, layer_weight, layer_bias, head_weight
):
    depth_b, rows_b, tile_len = stacks.shape
    depth_parts, row_parts = lax.axis_size("gz"), lax.axis_size("gy")
    parts = depth_parts * row_parts
    bricks = lax.axis_size("gx")
    assert (depth_b * depth_parts, rows_b * row_parts, parts * SLAB) == (NZ, NY, BX)
    assert depth_b == DEPTHS[-1] + 3
    smem = pl.BlockSpec(memory_space=pltpu.SMEM)
    pieces = pl.pallas_call(
        functools.partial(pack_kernel, parts=parts, bricks=bricks),
        out_shape=jax.ShapeDtypeStruct((parts * bricks * 3 * rows_b, 128), BF),
        in_specs=[smem, vmem()],
        out_specs=vmem(),
    )(offsets, stacks)
    pieces = lax.all_to_all(pieces, ("gz", "gy", "gx"), 0, 0, tiled=True)

    hbm = pl.BlockSpec(memory_space=pltpu.HBM)
    small = jax.ShapeDtypeStruct((24, 8 * C), F32)
    shapes = [jax.ShapeDtypeStruct((GROUPS[0] // 2, 384, 8 * C), BF)] + [
        jax.ShapeDtypeStruct(weight_shape(layer), BF) for layer in range(LAYERS)
    ]
    spaces = [pltpu.VMEM(shape.shape, shape.dtype) for shape in shapes]
    raw = (layer_weight, layer_bias, stem_weight, stem_bias[None], head_weight[None])
    rows, *weights = pl.pallas_call(
        weights_kernel,
        out_shape=[small] + shapes,
        in_specs=[hbm] * 5,
        out_specs=[vmem()] + [hbm] * 5,
        scratch_shapes=[pltpu.VMEM(array.shape, array.dtype) for array in raw]
        + spaces
        + [
            pltpu.VMEM((27, C, 4 * C), F32),
            pltpu.SemaphoreType.DMA((5,)),
            pltpu.SemaphoreType.DMA((5,)),
        ],
        compiler_params=pltpu.CompilerParams(vmem_limit_bytes=64 * 2**20 - 2**18),
        cost_estimate=pl.CostEstimate(flops=4000000, bytes_accessed=9000000, transcendentals=0),
    )(*raw)

    held = [max(act_rows(layer) for layer in range(odd, LAYERS, 2)) for odd in range(2)]
    scratch = (
        spaces
        + [pltpu.VMEM((2, NZ + 2, NY, 128), BF)]
        + [pltpu.VMEM((size, NY, 4 * C), BF) for size in held]
        + [pltpu.VMEM((NZ * NY // 2, 8 * C), F32)] * 2
        + [pltpu.SemaphoreType.DMA((5,))]
        + [pltpu.VMEM(edge_shape(layer), BF) for layer in range(PACKED)]
    )
    logits = pl.pallas_call(
        conv_kernel,
        out_shape=jax.ShapeDtypeStruct((parts, SLAB, 128), F32),
        in_specs=[smem, smem, vmem(), vmem()] + [hbm] * 5,
        out_specs=vmem(),
        scratch_shapes=scratch,
        compiler_params=pltpu.CompilerParams(vmem_limit_bytes=64 * 2**20 - 2**18),
        cost_estimate=pl.CostEstimate(
            flops=20000000000, bytes_accessed=9000000, transcendentals=0
        ),
    )(offsets, ramp_width, pieces, rows, *weights)
    logits = lax.all_to_all(logits, ("gz", "gy"), 0, 0, tiled=True)
    logits = logits[:, :, : depth_b * rows_b].transpose(2, 0, 1)
    return logits.reshape(depth_b, rows_b, BX)


def solution(mesh):
    return jax.shard_map(
        body,
        mesh=mesh,
        in_specs=(P("gz", "gy", "gx"), P(), P(), P(), P(), P(), P(), P()),
        out_specs=P("gz", "gy", "gx"),
        check_vma=False,
    )
```

```python
import functools
import math

import jax
import jax.numpy as jnp
from jax import lax
from jax.experimental import pallas as pl
from jax.experimental.pallas import tpu as pltpu
from jax.sharding import PartitionSpec as P

LAYERS = 4
H = 64
S = 32
BX = 128
C = 32
REACH = 16
SLAB = 8
WIDE = SLAB + 2 * REACH
NZ = 32
DEPTHS = (0, 3, 5)
NY = 32
GROUPS = (10, 5, 4, 3, 1)
PHASES = (1, 2, 2, 2, 2)
TAPS = (2, 2, 2, 3)
COLSTEP = (1, 1, 2, 4)
PACKED = 2
ORIGIN = (-15, -14, -12, -8, 0)
BF = jnp.bfloat16
F32 = jnp.float32


def repeated(row, copies):
    return jnp.concatenate([row] * copies, axis=1)


def weights_kernel(*refs):
    sources, rows_ref, outs, refs = refs[:5], refs[5], refs[6:11], refs[11:]
    inputs, built, turned, in_sems, out_sems = refs[:5], refs[5:10], *refs[10:]
    fetches = [
        pltpu.make_async_copy(a, b, in_sems.at[k]) for k, (a, b) in enumerate(zip(sources, inputs))
    ]
    stores = [
        pltpu.make_async_copy(a, b, out_sems.at[k]) for k, (a, b) in enumerate(zip(built, outs))
    ]
    for copy in fetches:
        copy.start()
    for copy in fetches:
        copy.wait()
    lw_ref, lb_ref, sw_ref, sb_ref, head_ref = inputs
    ws_ref, w_refs = built[0], built[1:]
    lane = lax.broadcasted_iota(jnp.int32, (C, 4 * C), 1) // C
    zero = jnp.zeros((C, 4 * C), BF)
    for layer in range(LAYERS):
        spacing = 2**layer
        out = w_refs[layer]
        flat = lw_ref[layer].astype(F32).reshape(27 * C, C)
        flat = jnp.concatenate([flat, jnp.zeros((28 * 4 * C - 27 * C, C), F32)], axis=0)
        flat = jnp.concatenate([flat, jnp.zeros((28 * 4 * C, 3 * C), F32)], axis=1)
        for t in range(27):
            turned[t] = flat[C * t : C * t + 4 * C].T[:C]

        def per_row_tap(s, carry, layer=layer, spacing=spacing, out=out):
            taps = []
            for c in range(3):
                taps.append([])
                for a in range(3):
                    block = jnp.where(lane == 0, turned[9 * c + a + 3 * s], 0.0)
                    block = block + pltpu.roll(block, 2 * C, 1)
                    taps[c].append(block + pltpu.roll(block, C, 1))
            def place(i, t, xi, b, block):
                lanes = slice(4 * C * b, 4 * C * (b + 1))
                if layer >= PACKED:
                    out[s, i, t, xi * C : (xi + 1) * C, lanes] = block
                elif i == 0:
                    out[s, t, xi * C : (xi + 1) * C, lanes] = block
                else:
                    first = 2 * C * (t % 2) + xi * C
                    out[s, 4 + t // 2, first : first + C, lanes] = block

            for i in range(TAPS[layer]):
                for xi in range(4 if i == 0 or layer >= PACKED else 2):
                    for c in range(3):
                        block = jnp.zeros((C, 4 * C), F32)
                        for a in range(3):
                            xo = 4 * i + xi - COLSTEP[layer] * a
                            if 0 <= xo < 4:
                                block = jnp.where(lane == xo, taps[c][a], block)
                        block = block.astype(BF)
                        for b in range(2):
                            place(i, c + b, xi, b, block)
                    place(i, 0, xi, 1, zero)
                    place(i, 3, xi, 0, zero)
            return carry

        lax.fori_loop(0, 3, per_row_tap, 0)
        stores[1 + layer].start()
    row = lax.broadcasted_iota(jnp.int32, (128, 8 * C), 0)
    column = lax.broadcasted_iota(jnp.int32, (128, 8 * C), 1) // C
    stem = repeated(sw_ref[...].astype(F32), 8)

    def per_tile(k, carry):
        diff = row - column - 8 * k
        for c in range(3):
            block = jnp.zeros((128, 8 * C), F32)
            for b in range(3):
                for a in range(3):
                    tap = 9 * c + 3 * b + a
                    block = jnp.where(diff == WIDE * b + a, stem[tap : tap + 1, :], block)
            ws_ref[k, 128 * c : 128 * (c + 1), :] = block.astype(BF)
        return carry

    lax.fori_loop(0, GROUPS[0] // 2, per_tile, 0)
    stores[0].start()
    rows_ref[...] = jnp.zeros(rows_ref.shape, F32)
    rows_ref[0:1, :] = repeated(sb_ref[...], 8)
    for layer in range(LAYERS):
        rows_ref[8 + layer : 9 + layer, :] = repeated(lb_ref[layer : layer + 1], 8)
    head = repeated(head_ref[...].astype(F32), 8)
    spot = lax.broadcasted_iota(jnp.int32, (8, 8 * C), 0)
    rows_ref[16:24, :] = jnp.where(spot == column[:8], head, 0.0)
    for copy in stores:
        copy.wait()


def pack_kernel(off_ref, stacks_ref, out_ref, *, parts, bricks):
    brick = lax.axis_index("gx")
    depth, height, tile_len = stacks_ref.shape
    rows = 3 * height
    values = stacks_ref[...].astype(F32).reshape(depth * height, tile_len)
    lane = lax.broadcasted_iota(jnp.int32, (rows, 128), 1)
    turned = []
    for other in range(bricks):
        first = other * BX - REACH - (brick * BX - H + off_ref[brick])
        turned.append(pltpu.roll(values, lax.rem(64 * tile_len - first, tile_len), 1))
    for j in range(parts):
        messages = []
        for moved in turned:
            blocks = []
            for k, z in enumerate(DEPTHS):
                block = moved[z * height : z * height + rows]
                by = (tile_len + WIDE * k - SLAB * j) % tile_len
                blocks.append(pltpu.roll(block, by, 1)[:, :128])
            later = jnp.where(lane < 2 * WIDE, blocks[1], blocks[2])
            messages.append(jnp.where(lane < WIDE, blocks[0], later))
        message = jnp.concatenate(messages, axis=0).astype(BF)
        out_ref[j * bricks * rows : (j + 1) * bricks * rows] = message


def blended_slab(off_ref, ramp_ref, pieces_ref, first_col, total_cols, depth_parts, row_parts):
    bricks = lax.axis_size("gx")
    lane = lax.broadcasted_iota(jnp.int32, (1, 128), 1)
    lane = jnp.where(lane < WIDE, lane, jnp.where(lane < 2 * WIDE, lane - WIDE, lane - 2 * WIDE))
    col = lane + (first_col - REACH)
    height = NY // row_parts
    pieces = pieces_ref[...].astype(F32)
    pieces = pieces.reshape(depth_parts, row_parts, bricks, 3 * height, 128)
    numerator = jnp.zeros((depth_parts, row_parts, 3 * height, 128), F32)
    denominator = jnp.zeros((1, 128), F32)
    for tile in range(bricks):
        tile_len = 2 * BX
        spot = col - (tile * BX - H + off_ref[tile])
        inside = (spot >= 0) & (spot < tile_len)
        width = ramp_ref[tile].astype(F32)
        spot = spot.astype(F32)
        weight = jnp.minimum(1.0, jnp.minimum((spot + 1.0) / width, (tile_len - spot) / width))
        weight = jnp.where(inside, weight, 0.0)
        denominator = denominator + weight
        numerator = numerator + pieces[:, :, tile] * weight
    good = (col >= 0) & (col < total_cols)
    result = jnp.where(good, numerator / jnp.where(good, denominator, 1.0), 0.0)
    blocks = []
    for k in range(3):
        block = result.reshape(-1, 128)
        if k:
            block = pltpu.roll(block, 128 - WIDE * k, 1)
        block = block.reshape(depth_parts, row_parts, 3, height, 128)
        blocks.append(block if k < 2 else block[:, :, 1:])
    image = jnp.concatenate(blocks, axis=2).transpose(0, 2, 1, 3, 4).reshape(NZ * NY, 128)
    lanes = lax.broadcasted_iota(jnp.int32, image.shape, 1)
    return jnp.where(lanes < WIDE, image, 0.0)


def shifted(value, by):
    planes = value.reshape(-1, NY, value.shape[1])
    blank = jnp.zeros((planes.shape[0], abs(by), value.shape[1]), value.dtype)
    if by > 0:
        moved = jnp.concatenate([blank, planes[:, : NY - by]], axis=1)
    else:
        moved = jnp.concatenate([planes[:, -by:], blank], axis=1)
    return moved.reshape(value.shape)


def weight_shape(layer):
    return (3, 6, 4 * C, 8 * C) if layer < PACKED else (3, TAPS[layer], 4, 4 * C, 8 * C)


def act_shape(layer):
    planes = NZ // 2 ** (layer + 1) + 2
    return (3, PHASES[layer], GROUPS[layer], 2, 2**layer, planes, NY, 4 * C)


def edge_shape(layer):
    planes = NZ // 2 ** (layer + 1) + 1
    return (3, PHASES[layer], GROUPS[layer] - 1, 2**layer, planes, NY, 4 * C)


def act_rows(layer):
    return math.prod(act_shape(layer)[:-2])


def conv_kernel(off_ref, ramp_ref, pieces_ref, rows_ref, *refs):
    built, out_ref, refs = refs[:5], refs[5], refs[6:]
    held, stem_in, spaces, accs = refs[:5], refs[5], refs[6:8], refs[8:10]
    sems, edges = refs[10], refs[11:]
    fetches = [
        pltpu.make_async_copy(a, b, sems.at[k]) for k, (a, b) in enumerate(zip(built, held))
    ]
    for copy in fetches:
        copy.start()
    ws_ref, w_refs = held[0], held[1:]
    acts = [
        spaces[layer % 2].at[0 : act_rows(layer)].reshape(act_shape(layer))
        for layer in range(LAYERS)
    ]
    depth_parts, row_parts = lax.axis_size("gz"), lax.axis_size("gy")
    slab = lax.axis_index("gz") * row_parts + lax.axis_index("gy")
    first_col = lax.axis_index("gx") * BX + slab * SLAB
    total_cols = lax.axis_size("gx") * BX

    def col_mask(start, step, width):
        lane = lax.broadcasted_iota(jnp.int32, (1, width * C), 1) // C
        col = step * lane + (first_col + start)
        return jnp.where((col >= 0) & (col < total_cols), 1.0, 0.0)

    def clear_edges(layer):
        spacing = 2**layer
        pad = jnp.zeros((3, spacing, NY, 4 * C), BF)
        for phase in range(PHASES[layer]):
            for g in range(GROUPS[layer]):
                acts[layer][:, phase, g, 1, :, 0] = pad
                acts[layer][:, phase, g, 0, :, NZ // (2 * spacing) + 1] = pad

    def store(layer, phase, group, start, length, value):
        spacing = 2**layer
        rows = slice(start, start + length)
        for s in range(3):
            part = value if s == 1 else shifted(value, spacing if s == 0 else -spacing)
            planes = part.astype(BF).reshape(length, -1, 2, NY, 4 * C)
            count = planes.shape[1]
            low, high = planes[:, :, 0], planes[:, :, 1]
            acts[layer][s, phase, group, 0, rows, 1 : 1 + count] = low
            acts[layer][s, phase, group, 1, rows, 1 : 1 + count] = high
            if layer < PACKED and group > 0:
                low, high = low[..., : 2 * C], high[..., : 2 * C]
                blank = jnp.zeros((length, 1, NY, 2 * C), BF)
                out = edges[layer]
                first = jnp.concatenate([blank, low[:, :1]], axis=-1)
                inner = jnp.concatenate([high[:, :-1], low[:, 1:]], axis=-1)
                last = jnp.concatenate([high[:, -1:], blank], axis=-1)
                out[s, phase, group - 1, rows, 0:1] = first
                out[s, phase, group - 1, rows, 1:count] = inner
                out[s, phase, group - 1, rows, count : count + 1] = last

    def store_plane(layer, phase, group, start, length, m, value):
        spacing = 2**layer
        for s in range(3):
            part = value if s == 1 else shifted(value, spacing if s == 0 else -spacing)
            planes = part.astype(BF).reshape(length, NY, 4 * C)
            acts[layer][s, phase, group, m % 2, start : start + length, 1 + m // 2] = planes

    clear_edges(0)
    clear_edges(1)
    image = blended_slab(
        off_ref, ramp_ref, pieces_ref, first_col, total_cols, depth_parts, row_parts
    )
    packed = shifted(image, 1)
    packed = packed + pltpu.roll(image, WIDE, 1)
    packed = packed + pltpu.roll(shifted(image, -1), 2 * WIDE, 1)
    coarse = packed.astype(BF)
    fine = (packed - coarse.astype(F32)).astype(BF)
    for part, value in enumerate((coarse, fine)):
        stem_in[part, 0] = jnp.zeros((NY, 128), BF)
        stem_in[part, NZ + 1] = jnp.zeros((NY, 128), BF)
        stem_in[part, 1 : NZ + 1] = value.reshape(NZ, NY, 128)

    def stem_dot(k):
        lhs = jnp.concatenate(
            [stem_in[p, c : c + NZ].reshape(NZ * NY, 128) for p in range(2) for c in range(3)],
            axis=1,
        )
        weights = jnp.concatenate([ws_ref[k], ws_ref[k]], axis=0)
        return jnp.dot(lhs, weights, preferred_element_type=F32)

    def stem_finish(k, acc):
        mask = col_mask(8 * k + ORIGIN[0], 1, 8)
        value = jnp.maximum(acc + rows_ref[0:1], 0.0) * mask
        store(0, 0, 2 * k, 0, 1, value[:, : 4 * C])
        store(0, 0, 2 * k + 1, 0, 1, value[:, 4 * C :])

    def group_dot(layer, phase, g):
        spacing = 2**layer
        count = NZ // (2 * spacing)
        rows = NZ * NY // 2
        pieces = []
        for s in range(3):
            for t in range(4):
                start = (t + 1) // 2
                piece = acts[layer][s, phase, g, 1 - t % 2, :, start : start + count]
                pieces.append(piece.reshape(rows, 4 * C))
            for start in range(2):
                piece = edges[layer][s, phase, g, :, start : start + count]
                pieces.append(piece.reshape(rows, 4 * C))
        lhs = jnp.concatenate(pieces, axis=1)
        weights = w_refs[layer][...].reshape(18 * 4 * C, 8 * C)
        return jnp.dot(lhs, weights, preferred_element_type=F32)

    def centred(layer, phase, g, b, planes, rows):
        near = [acts[layer][1, phase, g + i, b, :, planes].reshape(rows, 4 * C) for i in range(2)]
        pair = jnp.concatenate(near, axis=1)
        first = COLSTEP[layer] * C
        return pair[:, first : first + 4 * C].astype(F32)

    def group_values(layer, phase, g, acc, mask):
        count = NZ // (2 * 2**layer)
        bias = rows_ref[8 + layer : 9 + layer, : 4 * C]
        values = []
        for b in range(2):
            centre = centred(layer, phase, g, b, slice(1, 1 + count), NZ * NY // 2)
            half = acc[:, 4 * C * b : 4 * C * (b + 1)] + bias
            values.append(centre + jnp.maximum(half, 0.0) * mask)
        return values

    def split_store(k, left, right):
        for b in range(2):
            one = left[b]
            block = lax.broadcasted_iota(jnp.int32, one.shape, 1) // C
            up, far = pltpu.roll(one, 3 * C, 1), pltpu.roll(one, 2 * C, 1)
            even = jnp.where(block == 0, one, up)
            odd = jnp.where(block == 0, up, far)
            if right is None:
                even_end = odd_end = jnp.zeros_like(one)
            else:
                two = right[b]
                down, far = pltpu.roll(two, C, 1), pltpu.roll(two, 2 * C, 1)
                even_end = jnp.where(block == 2, far, down)
                odd_end = jnp.where(block == 2, down, two)
            store(1, 0, k, b, 1, jnp.where(block < 2, even, even_end))
            store(1, 1, k, b, 1, jnp.where(block < 2, odd, odd_end))

    def first_layer():
        left = None
        for g in range(GROUPS[0] - 1):
            mask = col_mask(4 * g + ORIGIN[1], 1, 4)
            values = group_values(0, 0, g, group_dot(0, 0, g), mask)
            if left is None:
                left = values
            else:
                split_store(g // 2, left, values)
                left = None
        split_store(GROUPS[1] - 1, left, None)

    def second_layer():
        order = [(phase, g) for phase in range(2) for g in range(GROUPS[2])]
        order.sort(key=lambda pair: pair[1] == GROUPS[2] - 1)
        for phase, g in order:
            mask = col_mask(8 * g + phase + ORIGIN[2], 2, 4)
            values = group_values(1, phase, g, group_dot(1, phase, g), mask)
            for b in range(2):
                store(2, phase, g, 2 * b, 2, values[b])

    def plane_dot(layer, m, first=0, groups=1):
        spacing = 2**layer
        taps = [t for t in range(4) if 0 < m + (t + 1) // 2 < NZ // (2 * spacing) + 1]
        pieces, weights = [], []
        for s in range(3):
            for i in range(TAPS[layer]):
                for t in taps:
                    piece = acts[layer][s, :, i + first : i + first + groups, 1 - t % 2, :, m + (t + 1) // 2]
                    pieces.append(piece.reshape(2 * groups * spacing * NY, 4 * C))
                    weights.append(w_refs[layer][s, i, t])
        return jnp.dot(
            jnp.concatenate(pieces, axis=1),
            jnp.concatenate(weights, axis=0),
            preferred_element_type=F32,
        )

    def plane_values(layer, m, phase, g, acc, first=0, groups=1):
        spacing = 2**layer
        rows = spacing * NY
        mask = col_mask(8 * g + phase + ORIGIN[layer + 1], 2, 4)
        bias = rows_ref[8 + layer : 9 + layer, : 4 * C]
        at = (phase * groups + g - first) * rows
        values = []
        for b in range(2):
            if COLSTEP[layer] < 4:
                centre = centred(layer, phase, g, b, 1 + m, rows)
            else:
                centre = acts[layer][1, phase, g + 1, b, :, 1 + m].reshape(rows, 4 * C).astype(F32)
            half = acc[at : at + rows, 4 * C * b : 4 * C * (b + 1)] + bias
            values.append(centre + jnp.maximum(half, 0.0) * mask)
        return values

    def plane_finish(layer, m, first, groups, acc):
        spacing = 2**layer
        for phase in range(2):
            for g in range(first, first + groups):
                values = plane_values(layer, m, phase, g, acc, first, groups)
                for b, value in enumerate(values):
                    store_plane(layer + 1, phase, g, spacing * b, spacing, m, value)

    def head_finish(m, acc):
        layer = LAYERS - 1
        spacing = 2**layer
        for phase in range(2):
            last = jnp.concatenate(plane_values(layer, m, phase, 0, acc), axis=1)
            last = last.reshape(spacing, row_parts, NY // row_parts, 8 * C)
            last = last.transpose(1, 0, 2, 3).reshape(spacing * NY, 8 * C).astype(BF)
            heads = lax.dot_general(
                rows_ref[16:24].astype(BF),
                last,
                (((1,), (1,)), ((), ())),
                preferred_element_type=F32,
            )
            size = spacing * NY // row_parts
            for y in range(row_parts):
                for b in range(2):
                    lanes = slice(size * phase, size * (phase + 1))
                    out_ref[(2 * m + b) * row_parts + y, :, lanes] = heads[
                        4 * b : 4 * b + 4, y * size : (y + 1) * size
                    ]

    fetches[0].wait()
    for k in range(GROUPS[0] // 2):
        if k == GROUPS[0] // 2 - 1:
            for copy in fetches[1:]:
                copy.wait()
        stem_finish(k, stem_dot(k))
    for layer in range(LAYERS):
        if layer == 0:
            first_layer()
        elif layer == 1:
            second_layer()
        elif layer == 2:
            for first, groups in ((0, GROUPS[3] - 1), (GROUPS[3] - 1, 1)):
                for m in range(NZ // 2 ** (layer + 1)):
                    plane_finish(layer, m, first, groups, plane_dot(layer, m, first, groups))
        else:
            for m in range(NZ // 2 ** (layer + 1)):
                accs[m][...] = plane_dot(layer, m)
                if m:
                    head_finish(m - 1, accs[m - 1])
            head_finish(m, accs[m])


def vmem():
    return pl.BlockSpec(memory_space=pltpu.VMEM)


def body(
    stacks, offsets, ramp_width, stem_weight, stem_bias, layer_weight, layer_bias, head_weight
):
    depth_b, rows_b, tile_len = stacks.shape
    depth_parts, row_parts = lax.axis_size("gz"), lax.axis_size("gy")
    parts = depth_parts * row_parts
    bricks = lax.axis_size("gx")
    assert (depth_b * depth_parts, rows_b * row_parts, parts * SLAB) == (NZ, NY, BX)
    assert depth_b == DEPTHS[-1] + 3
    smem = pl.BlockSpec(memory_space=pltpu.SMEM)
    pieces = pl.pallas_call(
        functools.partial(pack_kernel, parts=parts, bricks=bricks),
        out_shape=jax.ShapeDtypeStruct((parts * bricks * 3 * rows_b, 128), BF),
        in_specs=[smem, vmem()],
        out_specs=vmem(),
    )(offsets, stacks)
    pieces = lax.all_to_all(pieces, ("gz", "gy", "gx"), 0, 0, tiled=True)

    hbm = pl.BlockSpec(memory_space=pltpu.HBM)
    small = jax.ShapeDtypeStruct((24, 8 * C), F32)
    shapes = [jax.ShapeDtypeStruct((GROUPS[0] // 2, 384, 8 * C), BF)] + [
        jax.ShapeDtypeStruct(weight_shape(layer), BF) for layer in range(LAYERS)
    ]
    spaces = [pltpu.VMEM(shape.shape, shape.dtype) for shape in shapes]
    raw = (layer_weight, layer_bias, stem_weight, stem_bias[None], head_weight[None])
    rows, *weights = pl.pallas_call(
        weights_kernel,
        out_shape=[small] + shapes,
        in_specs=[hbm] * 5,
        out_specs=[vmem()] + [hbm] * 5,
        scratch_shapes=[pltpu.VMEM(array.shape, array.dtype) for array in raw]
        + spaces
        + [
            pltpu.VMEM((27, C, 4 * C), F32),
            pltpu.SemaphoreType.DMA((5,)),
            pltpu.SemaphoreType.DMA((5,)),
        ],
        compiler_params=pltpu.CompilerParams(vmem_limit_bytes=64 * 2**20 - 2**18),
        cost_estimate=pl.CostEstimate(flops=4000000, bytes_accessed=9000000, transcendentals=0),
    )(*raw)

    held = [max(act_rows(layer) for layer in range(odd, LAYERS, 2)) for odd in range(2)]
    scratch = (
        spaces
        + [pltpu.VMEM((2, NZ + 2, NY, 128), BF)]
        + [pltpu.VMEM((size, NY, 4 * C), BF) for size in held]
        + [pltpu.VMEM((NZ * NY // 2, 8 * C), F32)] * 2
        + [pltpu.SemaphoreType.DMA((5,))]
        + [pltpu.VMEM(edge_shape(layer), BF) for layer in range(PACKED)]
    )
    logits = pl.pallas_call(
        conv_kernel,
        out_shape=jax.ShapeDtypeStruct((parts, SLAB // 2, 128), F32),
        in_specs=[smem, smem, vmem(), vmem()] + [hbm] * 5,
        out_specs=vmem(),
        scratch_shapes=scratch,
        compiler_params=pltpu.CompilerParams(vmem_limit_bytes=64 * 2**20 - 2**18),
        cost_estimate=pl.CostEstimate(
            flops=20000000000, bytes_accessed=9000000, transcendentals=0
        ),
    )(offsets, ramp_width, pieces, rows, *weights)
    logits = lax.all_to_all(logits, ("gz", "gy"), 0, 0, tiled=True)
    logits = logits.reshape(BX, depth_b * rows_b).T
    return logits.reshape(depth_b, rows_b, BX)


def solution(mesh):
    return jax.shard_map(
        body,
        mesh=mesh,
        in_specs=(P("gz", "gy", "gx"), P(), P(), P(), P(), P(), P(), P()),
        out_specs=P("gz", "gy", "gx"),
        check_vma=False,
    )
```
